512 devices in a mesh: height: 128 (over x, z_lo, y), tile: 4 (over z_hi, core).
Axes of the slice: x: 4, y: 4, z: 16 (z_hi: 2, z_lo: 8; z = z_hi * 8 + z_lo), core: 2. Of those that a mesh axis runs over, the one named last changes fastest.
Arguments:
- pulse_panels: bfloat16 [128, 2, 8, 12288], P('height', None, None, 'tile'), may hold values from -6 to 6
- interp_weights: bfloat16 [128, 4, 16, 3, 128, 128], P('height', None, 'tile'), may hold values from -0.3125 to 0.3125
- range_blocks: int32 [128, 4, 16, 3], P('height', None, 'tile'), may hold values from 0 to 25
- sector_of_panel: int32 [128], replicated, may hold values from 0 to 3
- layer_cos: float32 [512, 128, 8], P('height'), may hold values from -1 to 1, as said below
- layer_sin: float32 [512, 128, 8], P('height'), may hold values from -1 to 1
- ground_cos: bfloat16 [128, 8, 2048], P(None, None, 'tile'), may hold values from -1 to 1, as said below
- ground_sin: bfloat16 [128, 8, 2048], P(None, None, 'tile'), may hold values from -1 to 1
- height_kernel: float32 [5], replicated, may hold values from 0.2 to 1
Outputs:
- image: float32 [2, 512, 2048], P(None, 'height', 'tile')
The draws below stay inside these ranges and needn't reach their ends.
Inputs may be any that keep to these rules, and one draw needn't show every extreme that they name: range_blocks[h, s, u, k] counts range blocks of 128 bins in the window of the tile holding subtile u, widened by one block on each side: 0 is the block just before the window. layer_cos and layer_sin are the cosine and sine of one angle. ground_cos and ground_sin are the cosine and sine of one angle.
All inputs are finite; a program needn't handle non-finite values.
Results may differ from the reference program's by a relative error of at most 0.0003.
Values may be sent and summed in bfloat16 or wider, within the bound.
A program may use at most 128 MiB of HBM per device.

```python
import math
import jax
import jax.numpy as jnp
from jax import lax

RANGE = 12288
PASSES = 8
SECTORS = 4
BR = 128
BG = 128
KMAX = 3
TAPS = 5
SUB_DEV = 4
LAY_DEV = 4
PANELS = 128
SLABS = 128
NZ = 512
SUBTILES = 16
GROUND = 2048
N_TILE = 4


def phase_angles(key, marker, shape):
    marker_key = jax.random.fold_in(key, marker)
    return jax.random.uniform(marker_key, shape, jnp.float32, -math.pi, math.pi)


def draw_layer_cos(key, part):
    angles = phase_angles(key, 11, (NZ, PANELS, PASSES))
    return jnp.cos(angles)


def draw_layer_sin(key, part):
    angles = phase_angles(key, 11, (NZ, PANELS, PASSES))
    return jnp.sin(angles)


def draw_ground_cos(key, part):
    angles = phase_angles(key, 23, (PANELS, PASSES, GROUND))
    return jnp.cos(angles).astype(jnp.bfloat16)


def draw_ground_sin(key, part):
    angles = phase_angles(key, 23, (PANELS, PASSES, GROUND))
    return jnp.sin(angles).astype(jnp.bfloat16)


def plant(entries, rng, smallest, high):
    place = [jax.random.randint(jax.random.fold_in(rng, axis), (), 0, length) for axis, length in enumerate(entries.shape)]
    main_axis = entries.shape.index(max(entries.shape))
    neighbour = place[:main_axis] + [(place[main_axis] + 1) % entries.shape[main_axis]] + place[main_axis + 1:]
    return entries.at[tuple(place)].set(smallest).at[tuple(neighbour)].set(high)


def block_levels(key, shape, cuts, low, largest):
    loudness, own = 1.0, jax.random.fold_in(key, 6)
    for dim, shards_of in cuts:
        heights = jnp.exp(jax.random.uniform(jax.random.fold_in(own, dim), (shards_of,), jnp.float32, low / len(cuts), largest / len(cuts)))
        loudness = loudness * jnp.repeat(heights, shape[dim] // shards_of).reshape([-1 if axis == dim else 1 for axis in range(len(shape))])
    return loudness


def noise(stream_key, dims, width, most, shards=(), kind=jnp.bfloat16):
    result = width * jax.random.normal(stream_key, dims, jnp.float32)
    if shards:
        result = result * block_levels(stream_key, dims, shards, -0.22, 0.18)
    return jnp.clip(result, -most, most).astype(kind)


def setup_inputs(seed: int = 0) -> dict:
    splits = jax.random.split(jax.random.key(seed), 10)
    pulse_panels = noise(splits[0], (PANELS, 2, PASSES, RANGE), 1.0, 6.0, ((0, 128), (3, 4)))
    interp_weights = noise(splits[1], (SLABS, SECTORS, SUBTILES, KMAX, BR, BG), (KMAX * BR) ** -0.5, 0.3125, ((0, 128), (2, 4)))
    range_blocks = plant(jax.random.randint(splits[2], (SLABS, SECTORS, SUBTILES, KMAX), 0, RANGE // (N_TILE * BR) + 2), jax.random.fold_in(splits[2], 1), 0, (RANGE // (N_TILE * BR) + 2) - 1).astype(jnp.int32)
    sector_of_panel = plant(jax.random.randint(splits[3], (PANELS,), 0, SECTORS), jax.random.fold_in(splits[3], 1), 0, SECTORS - 1).astype(jnp.int32)
    layer_cos = draw_layer_cos(jax.random.fold_in(splits[9], 71), 0)
    layer_sin = draw_layer_sin(jax.random.fold_in(splits[9], 71), 0)
    ground_cos = draw_ground_cos(jax.random.fold_in(splits[9], 71), 0)
    ground_sin = draw_ground_sin(jax.random.fold_in(splits[9], 71), 0)
    height_kernel = jnp.clip(jax.random.uniform(splits[8], (TAPS,), jnp.float32, 0.2, 1.0), 0.2, 1.0)
    return dict(pulse_panels=pulse_panels, interp_weights=interp_weights, range_blocks=range_blocks, sector_of_panel=sector_of_panel, layer_cos=layer_cos, layer_sin=layer_sin, ground_cos=ground_cos, ground_sin=ground_sin, height_kernel=height_kernel)


HIGHEST = lax.Precision.HIGHEST

def rotation(cosine_table, sine_table):
    upper_half = jnp.concatenate([cosine_table, -sine_table], axis=-1)
    lower_half = jnp.concatenate([sine_table, cosine_table], axis=-1)
    return jnp.concatenate([upper_half, lower_half], axis=-2)

def reference(pulse_panels, interp_weights, range_blocks, sector_of_panel, layer_cos, layer_sin, ground_cos, ground_sin, height_kernel):
    window_blocks = RANGE // (N_TILE * BR)
    margin = TAPS // 2
    scaling = 1.0 / math.sqrt(PASSES * PANELS)
    padded = jnp.pad(pulse_panels, ((0, 0), (0, 0), (0, 0), (BR, BR)))
    panel_rows = padded.reshape(PANELS, 2 * PASSES, RANGE // BR + 2, BR)
    tile_start = jnp.arange(SUBTILES, dtype=jnp.int32) // SUB_DEV * window_blocks
    slab_cos = layer_cos.reshape(SLABS, LAY_DEV, PANELS, PASSES)
    slab_sin = layer_sin.reshape(SLABS, LAY_DEV, PANELS, PASSES)

    def slab_focus(members):
        weights, blocks, cosine_slab, sine_slab = members
        weights = weights.astype(jnp.float32)
        global_blocks = (blocks + tile_start[None, :, None]).astype(jnp.int32)

        def advance(accumulated, panel):
            sector = sector_of_panel[panel]
            chosen_weights = lax.dynamic_index_in_dim(weights, sector, 0, keepdims=False)
            chosen_blocks = lax.dynamic_index_in_dim(global_blocks, sector, 0, keepdims=False)
            samples = lax.dynamic_index_in_dim(panel_rows, panel, 0, keepdims=False)
            picked = jnp.take(samples, chosen_blocks, axis=1).astype(jnp.float32)
            amplitude = jnp.einsum('cukr,ukrg->cug', picked, chosen_weights).reshape(2, PASSES, GROUND)
            real_part = amplitude[0]
            imag_part = amplitude[1]
            phase_cos = lax.dynamic_index_in_dim(ground_cos, panel, 0, keepdims=False).astype(jnp.float32)
            phase_sin = lax.dynamic_index_in_dim(ground_sin, panel, 0, keepdims=False).astype(jnp.float32)
            turned = jnp.concatenate([real_part * phase_cos - imag_part * phase_sin, real_part * phase_sin + imag_part * phase_cos], axis=0)
            rotate = rotation(lax.dynamic_index_in_dim(cosine_slab, panel, 1, keepdims=False), lax.dynamic_index_in_dim(sine_slab, panel, 1, keepdims=False))
            return (accumulated + jnp.dot(rotate, turned, precision=HIGHEST, preferred_element_type=jnp.float32), None)
        initial = jnp.zeros((2 * LAY_DEV, GROUND), jnp.float32)
        focused, _ = lax.scan(advance, initial, jnp.arange(PANELS, dtype=jnp.int32))
        return focused
    focused = lax.map(slab_focus, (interp_weights, range_blocks, slab_cos, slab_sin))
    volume = focused.reshape(SLABS, 2, LAY_DEV, GROUND).transpose(1, 0, 2, 3).reshape(2, NZ, GROUND)
    padded_volume = jnp.pad(volume, ((0, 0), (margin, margin), (0, 0)))
    image = jnp.zeros((2, NZ, GROUND), jnp.float32)
    for tap_index in range(TAPS):
        image = image + height_kernel[tap_index] * padded_volume[:, tap_index:tap_index + NZ]
    return image * scaling
```

```python
import functools
import math

import jax
import jax.numpy as jnp
from jax import lax
from jax.experimental import pallas as pl
from jax.experimental.pallas import tpu as pltpu
from jax.sharding import PartitionSpec as P

MESH = pl.DeviceIdType.MESH

NX, NZ, NY, NT = 4, 8, 4, 4
NH = NX * NZ * NY
HALF = NH // 2
PART = 12
BLOCKS = 26

RA_Z, RB_Z, RC_Z = 0, 8, 16
RA_L, RA_R, RA_F0, RA_F1 = 24, 32, 40, 48
RB_L, RB_R, RB_F0, RB_F1 = 56, 64, 72, 80
RB_M = 88
RA_M, RC_Y, RC_M = 120, 121, 125
RW = 126
R_COS, R_SIN, R_BLK, R_HI, R_LO = 130, 131, 132, 133, 134
RV = 135
SA_L, SB_L = 140, 148
N_SEM = 156


def kernel(
    x_ref, w_ref, blk_ref, blk_v, sector_ref, cos_ref, sin_ref, gc_ref, gs_ref, taps_ref, out_ref,
    data, w_own, w_far, blk_far, blk_smem, cos_far, sin_far, gcos, gsin, mask, rot, vol, vol_in,
    ssem, rsem, lsem,
):
    h, t = lax.axis_index("height"), lax.axis_index("tile")
    x, z, y = lax.div(h, NZ * NY), lax.rem(lax.div(h, NY), NZ), lax.rem(h, NY)
    half, xm = lax.div(x, 2), lax.rem(x, 2)

    def place(px, pz, py):
        return ((px * NZ + pz) * NY + py, t)

    y_up, y_dn, y_far = lax.rem(y + 1, NY), lax.rem(y + 3, NY), lax.rem(y + 2, NY)
    mate = place(x + 1 - 2 * xm, z, y)
    partner = place(3 - x, z, y)
    up, dn, opposite = place(x, z, y_up), place(x, z, y_dn), place(x, z, y_far)
    z_up, z_dn = place(x, z + 1, y), place(x, z - 1, y)
    hp = partner[0]

    def other(height):
        px = lax.div(height, NZ * NY)
        return (3 - px) * (NZ * NY) + lax.rem(height, NZ * NY)

    def edge(source, target, send_id, receive_id, device):
        return pltpu.make_async_remote_copy(
            src_ref=source, dst_ref=target, send_sem=ssem.at[send_id], recv_sem=rsem.at[receive_id],
            device_id=device, device_id_type=MESH,
        )

    def send(region, number, device, send_id=None):
        edge(region, region, number if send_id is None else send_id, number, device).start()

    def got(region, number):
        edge(region, region, 0, number, mate).wait_recv()

    def sent(region, number):
        edge(region, region, number, 0, mate).wait_send()

    def part_a(zi, yi):
        return data.at[pl.ds(0, PART), :, zi, yi]

    def half_a(m, zi, yi):
        return data.at[pl.ds(0, PART), m, zi, yi]

    def part_b(m, zi, yi):
        return data.at[pl.ds(PART, PART), m, zi, yi]

    def half_b(n, m, zi, yi):
        return data.at[pl.ds(PART + n * (PART // 2), PART // 2), m, zi, yi]

    def ends(m, zi, yi):
        return data.at[pl.ds(2 * PART, 2), m, zi, yi]

    def ends_line(m, yi):
        return data.at[pl.ds(2 * PART, 2), m, :, yi]

    def ends_plane(m):
        return data.at[pl.ds(2 * PART, 2), m]

    barrier = pltpu.get_barrier_semaphore()

    def greet(device):
        pl.semaphore_signal(barrier, inc=1, device_id=device, device_id_type=MESH)

    @pl.when(t > 0)
    def _():
        greet((h, t - 1))

    @pl.when(t < NT - 1)
    def _():
        greet((h, t + 1))

    @pl.when(h > 0)
    def _():
        greet((h - 1, t))
        greet((other(h - 1), t))

    @pl.when(h < NH - 1)
    def _():
        greet((h + 1, t))
        greet((other(h + 1), t))

    for device in (mate, partner, up, dn, opposite):
        greet(device)

    @pl.loop(1, NZ)
    def _(n):
        greet(place(x, lax.rem(z + n, NZ), y))

    local = [
        pltpu.make_async_copy(w_ref, w_own, lsem.at[0]),
        pltpu.make_async_copy(gc_ref.at[pl.ds(half * HALF, HALF)], gcos, lsem.at[1]),
        pltpu.make_async_copy(gs_ref.at[pl.ds(half * HALF, HALF)], gsin, lsem.at[2]),
    ]
    for copy in local:
        copy.start()
    for b in range(2 * PART):
        lanes = slice(b * 128, (b + 1) * 128)
        data[b, xm, z, y] = jnp.concatenate([x_ref[0, :, lanes], x_ref[1, :, lanes]], axis=0)

    @pl.when(t == 0)
    def _():
        data[2 * PART + 1, xm, z, y] = jnp.zeros((16, 128), jnp.bfloat16)

    @pl.when(t == NT - 1)
    def _():
        data[2 * PART, xm, z, y] = jnp.zeros((16, 128), jnp.bfloat16)

    def flag(condition):
        return jnp.where(condition, 1, 0)

    pl.semaphore_wait(
        barrier,
        5 + (NZ - 1) + flag(t > 0) + flag(t < NT - 1) + flag(h > 0) + flag(h < NH - 1) + flag(hp > 0) + flag(hp < NH - 1),
    )

    def spread(zi):
        send(part_b(xm, zi, y), RB_M + zi * NY + y, mate)
        send(part_b(xm, zi, y), RB_L + zi, up)
        send(part_b(xm, zi, y), RB_R + zi, dn)

    def spread_a(zi):
        send(part_a(zi, y), RA_L + zi, up)
        send(part_a(zi, y), RA_R + zi, dn)

    def to_z(region, number, left_id, rightward, leftward):
        @pl.when(rightward)
        def _():
            send(region, number, z_up)

        @pl.when(leftward)
        def _():
            send(region, number, z_dn, left_id)

    send(half_a(xm, z, y), RA_M, mate)
    to_z(part_b(xm, z, y), RB_Z + z, SB_L + z, z < NZ - 1, z > 0)
    spread(z)

    @pl.when(t < NT - 1)
    def _():
        edge(data.at[2 * PART - 1, xm, z, y], data.at[2 * PART + 1, xm, z, y], R_HI, R_HI, (h, t + 1)).start()

    @pl.when(t > 0)
    def _():
        edge(data.at[0, xm, z, y], data.at[2 * PART, xm, z, y], R_LO, R_LO, (h, t - 1)).start()

    edge(cos_ref, cos_far, R_COS, R_COS, partner).start()
    edge(sin_ref, sin_far, R_SIN, R_SIN, partner).start()
    edge(blk_v, blk_far, R_BLK, R_BLK, partner).start()
    for s in range(4):
        edge(w_ref.at[s], w_far.at[s], RW + s, RW + s, partner).start()
    got(half_a(1 - xm, z, y), RA_M)
    to_z(part_a(z, y), RA_Z + z, SA_L + z, z < NZ - 1, z > 0)
    spread_a(z)

    @pl.loop(0, HALF)
    def _(n):
        sector = sector_ref[half * HALF + n]
        for s in range(4):
            one = jnp.where(sector == s, 1.0, 0.0).astype(jnp.float32)
            mask[s, n] = jnp.full((16, 128), one, jnp.float32).astype(jnp.bfloat16)

    short = jnp.minimum(z, NZ - 1 - z)

    def order(k):
        paired = k <= 2 * short
        distance = jnp.where(paired, lax.div(k + 1, 2), k - short)
        from_dn = jnp.where(paired, lax.rem(k, 2) == 1, z > NZ - 1 - z)
        zi = jnp.where(k == 0, z, jnp.where(from_dn, z - distance, z + distance))
        return zi, from_dn

    @pl.loop(1, NZ + 2)
    def _(k):
        @pl.when(k < NZ)
        def _():
            zi, from_dn = order(k)
            rightward = jnp.logical_and(from_dn, z < NZ - 1)
            leftward = jnp.logical_and(jnp.logical_not(from_dn), z > 0)
            got(part_b(xm, zi, y), RB_Z + zi)
            to_z(part_b(xm, zi, y), RB_Z + zi, SB_L + zi, rightward, leftward)
            spread(zi)
            got(part_a(zi, y), RA_Z + zi)
            to_z(part_a(zi, y), RA_Z + zi, SA_L + zi, rightward, leftward)
            spread_a(zi)

        @pl.when(k <= NZ)
        def _():
            zi, _ = order(k - 1)
            got(part_b(xm, zi, y_dn), RB_L + zi)
            send(half_b(0, xm, zi, y_dn), RB_F0 + zi, up)
            send(part_b(xm, zi, y_dn), RB_M + zi * NY + y_dn, mate)
            got(part_b(xm, zi, y_up), RB_R + zi)
            send(half_b(1, xm, zi, y_up), RB_F1 + zi, dn)
            send(part_b(xm, zi, y_up), RB_M + zi * NY + y_up, mate)
            got(part_a(zi, y_dn), RA_L + zi)
            send(half_a(0, zi, y_dn), RA_F0 + zi, up)
            got(part_a(zi, y_up), RA_R + zi)
            send(half_a(1, zi, y_up), RA_F1 + zi, dn)

        @pl.when(k >= 2)
        def _():
            zi, _ = order(k - 2)
            got(half_b(0, xm, zi, y_far), RB_F0 + zi)
            got(half_b(1, xm, zi, y_far), RB_F1 + zi)
            send(part_b(xm, zi, y_far), RB_M + zi * NY + y_far, mate)

        @pl.when(k == 2)
        def _():
            @pl.when(t > 0)
            def _():
                got(data.at[2 * PART + 1, xm, z, y], R_HI)

            @pl.when(t < NT - 1)
            def _():
                got(data.at[2 * PART, xm, z, y], R_LO)

            @pl.loop(1, NZ)
            def _(n):
                zn = lax.rem(z + n, NZ)
                send(ends(xm, z, y), RC_Z + z, place(x, zn, y), RC_Z + zn)

        @pl.when(k == 4)
        def _():
            @pl.loop(1, NZ)
            def _(n):
                zn = lax.rem(z + n, NZ)
                got(ends(xm, zn, y), RC_Z + zn)

            send(ends_line(xm, y), RC_Y + y, up, RC_Y + y_up)
            send(ends_line(xm, y), RC_Y + y, dn, RC_Y + y_dn)
            send(ends_line(xm, y), RC_Y + y, opposite, RC_Y + y_far)

        @pl.when(k == 6)
        def _():
            for yi in (y_up, y_dn, y_far):
                got(ends_line(xm, yi), RC_Y + yi)
            send(ends_plane(xm), RC_M, mate)

    got(cos_far, R_COS)
    got(sin_far, R_SIN)
    got(blk_far, R_BLK)
    blocks_in = pltpu.make_async_copy(blk_far, blk_smem, lsem.at[3])
    blocks_in.start()
    lane = lax.broadcasted_iota(jnp.int32, (NH, HALF * 16), 1)
    panel = lax.broadcasted_iota(jnp.int32, (NH, HALF * 16), 0)
    expand = (lax.shift_right_logical(lane, 4) + half * HALF == panel).astype(jnp.float32).astype(jnp.bfloat16)
    row = jnp.bitwise_and(lax.broadcasted_iota(jnp.int32, (128, HALF * 16), 0), 15)
    column = jnp.bitwise_and(lax.broadcasted_iota(jnp.int32, (128, HALF * 16), 1), 15)
    for slab, (cosine, sine) in enumerate(((cos_ref, sin_ref), (cos_far, sin_far))):
        rows = []
        for layer in range(4):
            rows += [cosine[layer], -sine[layer]]
        for layer in range(4):
            rows += [sine[layer], cosine[layer]]
        table = jnp.concatenate(rows, axis=0)
        high = table.astype(jnp.bfloat16)
        low = (table - high.astype(jnp.float32)).astype(jnp.bfloat16)
        halves = []
        for piece in (high, low):
            wide = jnp.dot(piece, expand, preferred_element_type=jnp.float32)
            wide = jnp.where(row == column, wide, 0.0)
            halves.append(jnp.sum(wide.reshape(8, 16, HALF * 16), axis=1))
        rot[slab] = jnp.concatenate(halves, axis=0).astype(jnp.bfloat16)
    blocks_in.wait()
    for copy in local:
        copy.wait()

    @pl.loop(0, NZ)
    def _(zi):
        for yi in range(NY):
            got(part_b(1 - xm, zi, yi), RB_M + zi * NY + yi)
        got(half_a(0, zi, y_far), RA_F0 + zi)
        got(half_a(1, zi, y_far), RA_F1 + zi)

    got(ends_plane(1 - xm), RC_M)
    for s in range(4):
        got(w_far.at[s], RW + s)

    def focus(slab, weights, blocks):
        vol[slab] = jnp.zeros((8, 512), jnp.float32)

        @pl.loop(0, 16)
        def _(i):
            group, u = lax.div(i, 4), lax.rem(i, 4)
            lanes = pl.ds(pl.multiple_of(u * 128, 128), 128)
            panels = pl.ds(pl.multiple_of(group * 16, 16), 16)
            pieces = []
            for s in range(4):
                chosen = mask[s, panels]
                for k in range(3):
                    place_of = lax.rem(blocks[k, s, u] + (BLOCKS - 1), BLOCKS)
                    picked = data[place_of, lax.div(group, 2), pl.ds(lax.rem(group, 2) * 4, 4)]
                    pieces.append((picked.reshape(16, 16, 128) * chosen).reshape(256, 128))
            amplitude = jnp.dot(
                jnp.concatenate(pieces, axis=1), weights[:, u].reshape(12 * 128, 128),
                preferred_element_type=jnp.float32,
            ).reshape(16, 2, 8, 128)
            re, im = amplitude[:, 0], amplitude[:, 1]
            pc = gcos[panels, :, lanes].astype(jnp.float32)
            ps = gsin[panels, :, lanes].astype(jnp.float32)
            turned = jnp.concatenate([re * pc - im * ps, re * ps + im * pc], axis=1).reshape(256, 128)
            high = turned.astype(jnp.bfloat16)
            low = (turned - high.astype(jnp.float32)).astype(jnp.bfloat16)
            rotate = rot[slab, :, pl.ds(pl.multiple_of(group * 256, 256), 256)]
            layers = jnp.dot(rotate, high, preferred_element_type=jnp.float32)
            layers = layers + jnp.dot(rotate, low, preferred_element_type=jnp.float32)
            vol[slab, :, lanes] += layers[:8] + layers[8:]

    def give(slab, slot, device):
        edge(vol.at[slab], vol_in.at[slot], RV + slot, RV + slot, device).start()

    focus(1, w_far, blk_smem)
    give(1, 0, partner)

    @pl.when(hp < NH - 1)
    def _():
        give(1, 3, (hp + 1, t))

    @pl.when(hp > 0)
    def _():
        give(1, 4, (hp - 1, t))

    focus(0, w_own, blk_ref)

    @pl.when(h < NH - 1)
    def _():
        give(0, 1, (h + 1, t))

    @pl.when(h > 0)
    def _():
        give(0, 2, (h - 1, t))

    def take(slot):
        got(vol_in.at[slot], RV + slot)

    @pl.when(h > 0)
    def _():
        take(1)
        take(3)

    @pl.when(h == 0)
    def _():
        vol_in[1] = jnp.zeros((8, 512), jnp.float32)
        vol_in[3] = jnp.zeros((8, 512), jnp.float32)

    @pl.when(h < NH - 1)
    def _():
        take(2)
        take(4)

    @pl.when(h == NH - 1)
    def _():
        vol_in[2] = jnp.zeros((8, 512), jnp.float32)
        vol_in[4] = jnp.zeros((8, 512), jnp.float32)

    take(0)
    here = vol[0] + vol_in[0]
    below = vol_in[1] + vol_in[3]
    above = vol_in[2] + vol_in[4]
    for part in range(2):
        rows = jnp.concatenate(
            [below[4 * part + 2 : 4 * part + 4], here[4 * part : 4 * part + 4], above[4 * part : 4 * part + 2]], axis=0
        )
        image = jnp.zeros((4, 512), jnp.float32)
        for j in range(5):
            image = image + taps_ref[j] * rows[j : j + 4]
        out_ref[part] = image * (1.0 / math.sqrt(8 * NH))

    @pl.loop(0, NZ)
    def _(k):
        zi, from_dn = order(k)
        own = k == 0
        rightward = jnp.logical_and(jnp.logical_or(own, from_dn), z < NZ - 1)
        leftward = jnp.logical_and(jnp.logical_or(own, jnp.logical_not(from_dn)), z > 0)

        @pl.when(rightward)
        def _():
            sent(part_b(xm, zi, y), RB_Z + zi)
            sent(part_a(zi, y), RA_Z + zi)

        @pl.when(leftward)
        def _():
            sent(part_b(xm, zi, y), SB_L + zi)
            sent(part_a(zi, y), SA_L + zi)

        for number in (RB_L, RB_R):
            sent(part_b(xm, zi, y), number + zi)
        for number in (RA_L, RA_R):
            sent(part_a(zi, y), number + zi)
        for n in range(2):
            sent(half_b(n, xm, zi, y), RB_F0 + 8 * n + zi)
            sent(half_a(n, zi, y), RA_F0 + 8 * n + zi)
        for yi in range(NY):
            sent(part_b(xm, zi, yi), RB_M + zi * NY + yi)

    sent(half_a(xm, z, y), RA_M)

    @pl.loop(1, NZ)
    def _(n):
        sent(ends(xm, z, y), RC_Z + lax.rem(z + n, NZ))

    for yi in (y_up, y_dn, y_far):
        sent(ends_line(xm, y), RC_Y + yi)
    sent(ends_plane(xm), RC_M)
    for s in range(4):
        sent(w_far.at[s], RW + s)
    sent(cos_far, R_COS)
    sent(sin_far, R_SIN)
    sent(blk_far, R_BLK)

    @pl.when(t < NT - 1)
    def _():
        sent(data.at[0, xm, z, y], R_HI)

    @pl.when(t > 0)
    def _():
        sent(data.at[0, xm, z, y], R_LO)

    sent(vol.at[0], RV)
    for slot, condition in ((1, h < NH - 1), (2, h > 0), (3, hp < NH - 1), (4, hp > 0)):

        @pl.when(condition)
        def _():
            sent(vol.at[0], RV + slot)


def local(pulse_panels, interp_weights, range_blocks, sector_of_panel, layer_cos, layer_sin, ground_cos, ground_sin, height_kernel):
    blocks = jnp.transpose(range_blocks[0], (2, 0, 1))
    vmem, smem, anywhere = (pl.BlockSpec(memory_space=space) for space in (pltpu.VMEM, pltpu.SMEM, pl.ANY))
    f32, bf16, i32 = jnp.float32, jnp.bfloat16, jnp.int32
    return pl.pallas_call(
        kernel,
        out_shape=jax.ShapeDtypeStruct((2, 4, 512), f32),
        in_specs=[vmem, anywhere, smem, vmem, smem, vmem, vmem, anywhere, anywhere, smem],
        out_specs=vmem,
        scratch_shapes=[
            pltpu.VMEM((BLOCKS, 2, NZ, NY, 16, 128), bf16),
            pltpu.VMEM((4, 4, 3, 128, 128), bf16),
            pltpu.VMEM((4, 4, 3, 128, 128), bf16),
            pltpu.VMEM((3, 4, 4), i32),
            pltpu.SMEM((3, 4, 4), i32),
            pltpu.VMEM((4, 8, NH), f32),
            pltpu.VMEM((4, 8, NH), f32),
            pltpu.VMEM((HALF, 8, 512), bf16),
            pltpu.VMEM((HALF, 8, 512), bf16),
            pltpu.VMEM((4, HALF, 16, 128), bf16),
            pltpu.VMEM((2, 16, HALF * 16), bf16),
            pltpu.VMEM((2, 8, 512), f32),
            pltpu.VMEM((5, 8, 512), f32),
            pltpu.SemaphoreType.DMA((N_SEM,)),
            pltpu.SemaphoreType.DMA((N_SEM,)),
            pltpu.SemaphoreType.DMA((4,)),
        ],
        compiler_params=pltpu.CompilerParams(collective_id=0, has_side_effects=True, vmem_limit_bytes=48 << 20),
        name="focus",
    )(
        pulse_panels[0], interp_weights[0], blocks, blocks, sector_of_panel,
        jnp.swapaxes(layer_cos, 1, 2), jnp.swapaxes(layer_sin, 1, 2), ground_cos, ground_sin, height_kernel,
    )


def solution(mesh):
    in_specs = (
        P("height", None, None, "tile"),
        P("height", None, "tile", None, None, None),
        P("height", None, "tile", None),
        P(),
        P("height", None, None),
        P("height", None, None),
        P(None, None, "tile"),
        P(None, None, "tile"),
        P(),
    )
    return jax.shard_map(local, mesh=mesh, in_specs=in_specs, out_specs=P(None, "height", "tile"), check_vma=False)
```

```python
import math

import jax
import jax.numpy as jnp
from jax import lax
from jax.experimental import pallas as pl
from jax.experimental.pallas import tpu as pltpu
from jax.sharding import PartitionSpec as P

MESH = pl.DeviceIdType.MESH

NX, NZ, NY, NT = 4, 8, 4, 4
NH = NX * NZ * NY
HALF = NH // 2
WINDOW = 24
BLOCKS = WINDOW + 2
PART = 10
GROUPS = NZ // 2

A_MATE, B_Z, A_Z, B_DN, B_UP, B_FAR, A_DN, A_UP, ENDS, ENDS_MATE, ENDS_Z, FOCUS = range(12)
ORDER = (
    (A_MATE, 0), (B_Z, 1), (B_DN, 0), (B_UP, 0), (B_Z, 2), (ENDS, 0), (A_Z, 1), (A_DN, 0), (A_UP, 0), (B_DN, 1),
    (B_UP, 1), (B_Z, 4), (B_Z, 3), (B_FAR, 0), (A_Z, 2), (B_DN, 2), (B_UP, 2), (A_DN, 1), (A_UP, 1), (B_Z, 5),
    (B_FAR, 1), (A_Z, 3), (B_Z, 6), (B_DN, 4), (B_UP, 4), (A_Z, 4), (B_DN, 3), (B_UP, 3), (A_DN, 2), (A_UP, 2),
    (B_FAR, 2), (B_Z, 7), (ENDS_MATE, 0), (A_Z, 5), (B_DN, 5), (B_UP, 5), (A_DN, 3), (A_UP, 3), (A_Z, 6), (B_DN, 6),
    (ENDS_Z, 0), (B_UP, 6), (B_FAR, 4), (A_DN, 4), (A_UP, 4), (B_FAR, 3), (A_Z, 7), (B_DN, 7), (B_UP, 7),
    (FOCUS, 0, 0), (A_DN, 5), (A_UP, 5), (B_FAR, 5), (FOCUS, 0, 1), (A_DN, 6), (A_UP, 6), (B_FAR, 6), (FOCUS, 1, 0),
    (FOCUS, 1, 1), (A_DN, 7), (A_UP, 7), (B_FAR, 7), (FOCUS, 2, 0), (FOCUS, 2, 1), (FOCUS, 3, 1), (FOCUS, 3, 0),
)
ONWARD = {0: (4, 2, 1), 4: (2, 1), 2: (1,), 6: (1,)}
N_SEND, N_RECEIVE, N_LOCAL = 256, 224, 24


def kernel(
    x_hbm, w_ref, blk_hbm, sector_hbm, cos_hbm, sin_hbm, gc_ref, gs_ref, taps_hbm, out_ref,
    x_ref, blk_v, blk_ref, sector_ref, cos_ref, sin_ref, taps_ref, data0, data1, data2, data3,
    w_own, w_far, blk_far, blk_smem, cos_far, sin_far, gcos, gsin, mask, rot, vol, vol_in,
    ssem, rsem, lsem, ready,
):
    data = (data0, data1, data2, data3)
    h, t = lax.axis_index("height"), lax.axis_index("tile")
    x, z, y = lax.div(h, NZ * NY), lax.rem(lax.div(h, NY), NZ), lax.rem(h, NY)
    half, xm = lax.div(x, 2), lax.rem(x, 2)

    def place(px, pz, py):
        return ((px * NZ + pz) * NY + py, t)

    def z_at(distance):
        flipped = z
        for bit in (1, 2, 4):
            if distance & bit:
                flipped = flipped + bit - 2 * bit * lax.rem(lax.div(z, bit), 2)
        return flipped

    y_up, y_dn, y_far = lax.rem(y + 1, NY), lax.rem(y + 3, NY), lax.rem(y + 2, NY)
    mate = place(x + 1 - 2 * xm, z, y)
    partner = place(3 - x, z, y)
    up, dn, opposite = place(x, z, y_up), place(x, z, y_dn), place(x, z, y_far)
    along = [place(x, z_at(d), y) for d in range(NZ)]
    hp = partner[0]

    receive_ids, sends = {}, []

    def receive_id(key):
        return receive_ids.setdefault(key, len(receive_ids))

    def edge(source, target, send_id, key, device):
        return pltpu.make_async_remote_copy(
            src_ref=source, dst_ref=target, send_sem=ssem.at[send_id], recv_sem=rsem.at[receive_id(key)],
            device_id=device, device_id_type=MESH,
        )

    def send(source, key, device, target=None, condition=None):
        number = len(sends)
        sends.append((source, condition))
        copy = edge(source, source if target is None else target, number, key, device)
        if condition is None:
            copy.start()
        else:
            pl.when(condition)(copy.start)

    def got(region, key):
        edge(region, region, 0, key, mate).wait_recv()

    retired = [0, 0]

    def retire():
        for number in range(*retired):
            source, condition = sends[number]
            copy = edge(source, source, number, ("a_mate",), mate)
            if condition is None:
                copy.wait_send()
            else:
                pl.when(condition)(copy.wait_send)
        retired[:] = [retired[1], len(sends)]

    def part_a(o, yi):
        return data[o // 2].at[pl.ds(0, PART), o % 2, :, yi]

    def half_a(m, o, yi):
        return data[o // 2].at[pl.ds(0, PART), o % 2, m, yi]

    def part_b(m, o, yi):
        return data[o // 2].at[pl.ds(PART, WINDOW - PART), o % 2, m, yi]

    def half_b(n, o, yi):
        size = (WINDOW - PART) // 2
        return data[o // 2].at[pl.ds(PART + n * size, size), o % 2, xm, yi]

    def ends(o, yi):
        return data[o // 2].at[pl.ds(WINDOW, 2), o % 2, :, yi]

    def ends_all(g, yi):
        return data[g].at[pl.ds(WINDOW, 2), :, :, yi]

    def own(block):
        return data0.at[block, 0, xm, y]

    barrier = pltpu.get_barrier_semaphore()

    def greet(device):
        pl.semaphore_signal(barrier, inc=1, device_id=device, device_id_type=MESH)

    @pl.when(t > 0)
    def _():
        greet((h, t - 1))

    @pl.when(t < NT - 1)
    def _():
        greet((h, t + 1))

    near = [along[4], along[2], along[1], opposite, up, dn, mate, partner]
    for device in near:
        greet(device)

    local_copies = [
        (w_ref, w_own), (sector_hbm, sector_ref), (taps_hbm, taps_ref), (blk_hbm, blk_ref),
    ]
    for o in range(NZ):
        local_copies += [(gc_ref.at[half, :, z_at(o)], gcos.at[o]), (gs_ref.at[half, :, z_at(o)], gsin.at[o])]
    first_copies = [(x_hbm, x_ref), (blk_hbm, blk_v), (cos_hbm, cos_ref), (sin_hbm, sin_ref)]
    copies = [
        pltpu.make_async_copy(source, target, lsem.at[n]) for n, (source, target) in enumerate(first_copies + local_copies)
    ]
    for copy in copies:
        copy.start()
    for copy in copies[: len(first_copies)]:
        copy.wait()
    for b in range(WINDOW):
        lanes = slice(b * 128, (b + 1) * 128)
        data0[b, 0, xm, y] = jnp.concatenate([x_ref[0, :, lanes], x_ref[1, :, lanes]], axis=0)

    @pl.when(t == 0)
    def _():
        data0[WINDOW + 1, 0, xm, y] = jnp.zeros((16, 128), jnp.bfloat16)

    @pl.when(t == NT - 1)
    def _():
        data0[WINDOW, 0, xm, y] = jnp.zeros((16, 128), jnp.bfloat16)

    edges = len(near) + jnp.where(t > 0, 1, 0) + jnp.where(t < NT - 1, 1, 0)
    pl.semaphore_wait(barrier, edges)

    def spread_b(o):
        for d in ONWARD.get(o, ()):
            send(part_b(xm, o, y), ("bz", o ^ d), along[d], part_b(xm, o ^ d, y))
        send(part_b(xm, o, y), ("b_dn", o), up)
        send(part_b(xm, o, y), ("b_up", o), dn)
        send(part_b(xm, o, y), ("b_mate", o, 0), mate)

    def spread_a(o):
        for d in ONWARD.get(o, ()):
            send(part_a(o, y), ("az", o ^ d), along[d], part_a(o ^ d, y))
        send(part_a(o, y), ("a_dn", o), up)
        send(part_a(o, y), ("a_up", o), dn)

    send(half_a(xm, 0, y), ("a_mate",), mate)
    spread_b(0)
    send(own(WINDOW - 1), ("right",), (h, t + 1), own(WINDOW + 1), t < NT - 1)
    send(own(0), ("left",), (h, t - 1), own(WINDOW), t > 0)
    send(cos_ref, ("cos",), partner, cos_far)
    send(sin_ref, ("sin",), partner, sin_far)
    send(blk_v, ("blocks",), partner, blk_far)
    for s in range(4):
        send(w_ref.at[s], ("weights", s), partner, w_far.at[s])

    def rotation(slab, cosine, sine):
        wide_shape = (NH, HALF * 16)
        column = lax.broadcasted_iota(jnp.int32, wide_shape, 1)
        row = lax.broadcasted_iota(jnp.int32, wide_shape, 0)
        z_of = lax.shift_right_logical(column, 7)
        z_of = jnp.bitwise_xor(z_of, jnp.full(wide_shape, z, jnp.int32))
        x_of = jnp.bitwise_and(lax.shift_right_logical(column, 6), 1) + 2 * half
        y_of = jnp.bitwise_and(lax.shift_right_logical(column, 4), 3)
        expand = ((x_of * NZ + z_of) * NY + y_of == row).astype(jnp.float32).astype(jnp.bfloat16)
        same = jnp.bitwise_and(column, 15) == jnp.bitwise_and(row, 15)
        rows = []
        for layer in range(4):
            rows += [cosine[layer], -sine[layer]]
        for layer in range(4):
            rows += [sine[layer], cosine[layer]]
        table = jnp.concatenate(rows, axis=0)
        high = table.astype(jnp.bfloat16)
        low = (table - high.astype(jnp.float32)).astype(jnp.bfloat16)
        halves = []
        for piece in (high, low):
            wide = jnp.dot(piece, expand, preferred_element_type=jnp.float32)
            wide = jnp.where(same, wide, 0.0)
            halves.append(jnp.sum(wide.reshape(8, 16, HALF * 16), axis=1))
        rot[slab] = jnp.concatenate(halves, axis=0).astype(jnp.bfloat16)

    rotation(0, cos_ref, sin_ref)
    for copy in copies[len(first_copies) :]:
        copy.wait()

    for o in range(NZ):

        @pl.loop(0, 2 * NY)
        def _(n):
            m, yi = lax.div(n, NY), lax.rem(n, NY)
            sector = sector_ref[((2 * half + m) * NZ + z_at(o)) * NY + yi]
            for s in range(4):
                one = jnp.where(sector == s, 1.0, 0.0).astype(jnp.float32)
                mask[s, o, m, yi] = jnp.full((16, 128), one, jnp.float32).astype(jnp.bfloat16)

    for slab in range(2):
        vol[slab] = jnp.zeros((8, 512), jnp.float32)

    def focus(g, slab):
        weights, blocks = ((w_own, blk_ref), (w_far, blk_smem))[slab]
        rotate = rot[slab, :, g * 256 : (g + 1) * 256]
        chosen = [mask[s, 2 * g : 2 * g + 2].reshape(16, 16, 128) for s in range(4)]
        for u in range(4):
            lanes = slice(u * 128, (u + 1) * 128)
            pieces = []
            for s in range(4):
                for k in range(3):
                    picked = data[g][lax.rem(blocks[k, s, u] + (BLOCKS - 1), BLOCKS)]
                    pieces.append((picked.reshape(16, 16, 128) * chosen[s]).reshape(256, 128))
            amplitude = jnp.dot(
                jnp.concatenate(pieces, axis=1), weights[:, u].reshape(12 * 128, 128),
                preferred_element_type=jnp.float32,
            ).reshape(16, 2, 8, 128)
            re, im = amplitude[:, 0], amplitude[:, 1]
            pc = gcos[2 * g : 2 * g + 2, :, :, :, lanes].reshape(16, 8, 128).astype(jnp.float32)
            ps = gsin[2 * g : 2 * g + 2, :, :, :, lanes].reshape(16, 8, 128).astype(jnp.float32)
            turned = jnp.concatenate([re * pc - im * ps, re * ps + im * pc], axis=1).reshape(256, 128)
            high = turned.astype(jnp.bfloat16)
            low = (turned - high.astype(jnp.float32)).astype(jnp.bfloat16)
            layers = jnp.dot(rotate, high, preferred_element_type=jnp.float32)
            layers = layers + jnp.dot(rotate, low, preferred_element_type=jnp.float32)
            vol[slab, :, lanes] += layers[:8] + layers[8:]

    complete, far_ready, told = set(), [], []

    def finish(g):
        if g in complete:
            return
        complete.add(g)
        for o in (2 * g, 2 * g + 1):
            for n, yi in enumerate((y, y_dn, y_up, y_far)):
                got(part_b(1 - xm, o, yi), ("b_mate", o, n))
            for m in range(2):
                got(half_a(m, o, y_far), ("a_far", m, o))
        for n, yi in enumerate((y_dn, y_up, y_far)):
            got(ends_all(g, yi), ("ends", n, g))

    def weights_from_afar():
        if far_ready:
            return
        got(cos_far, ("cos",))
        got(sin_far, ("sin",))
        got(blk_far, ("blocks",))
        copy = pltpu.make_async_copy(blk_far, blk_smem, lsem.at[N_LOCAL - 1])
        copy.start()
        rotation(1, cos_far, sin_far)
        copy.wait()
        for s in range(4):
            got(w_far.at[s], ("weights", s))
        far_ready.append(True)

    def give(slab, slot, device, condition=None):
        send(vol.at[slab], ("volume", slot), device, vol_in.at[slot], condition)

    for what, o, *more in ORDER:
        if what == A_MATE:
            got(half_a(1 - xm, 0, y), ("a_mate",))
            spread_a(0)
        elif what == B_Z:
            got(part_b(xm, o, y), ("bz", o))
            spread_b(o)
        elif what == A_Z:
            got(part_a(o, y), ("az", o))
            spread_a(o)
        elif what == B_DN:
            got(part_b(xm, o, y_dn), ("b_dn", o))
            send(half_b(0, o, y_dn), ("b_far", 0, o), up)
            send(part_b(xm, o, y_dn), ("b_mate", o, 1), mate)
        elif what == B_UP:
            got(part_b(xm, o, y_up), ("b_up", o))
            send(half_b(1, o, y_up), ("b_far", 1, o), dn)
            send(part_b(xm, o, y_up), ("b_mate", o, 2), mate)
        elif what == B_FAR:
            for n in range(2):
                got(half_b(n, o, y_far), ("b_far", n, o))
            send(part_b(xm, o, y_far), ("b_mate", o, 3), mate)
        elif what == A_DN:
            got(part_a(o, y_dn), ("a_dn", o))
            send(half_a(0, o, y_dn), ("a_far", 0, o), up)
        elif what == A_UP:
            got(part_a(o, y_up), ("a_up", o))
            send(half_a(1, o, y_up), ("a_far", 1, o), dn)
        elif what == ENDS:
            pl.when(t > 0)(lambda: got(own(WINDOW + 1), ("right",)))
            pl.when(t < NT - 1)(lambda: got(own(WINDOW), ("left",)))
            mine = data0.at[pl.ds(WINDOW, 2), 0, xm, y]
            send(mine, ("ends_mate",), mate)
        elif what == ENDS_MATE:
            got(data0.at[pl.ds(WINDOW, 2), 0, 1 - xm, y], ("ends_mate",))
            for d in range(NZ - 1, 0, -1):
                send(ends(0, y), ("ends_z", d), along[d], ends(d, y))
        elif what == ENDS_Z:
            for d in range(1, NZ):
                got(ends(d, y), ("ends_z", d))
            for g in range(GROUPS):
                for n, device in enumerate((up, dn, opposite)):
                    send(ends_all(g, y), ("ends", n, g), device)
        elif what == FOCUS:
            finish(o)
            if more[0] == 1:
                weights_from_afar()
            if len(complete) == GROUPS and not told:
                pl.semaphore_signal(ready, inc=1, device_id=partner, device_id_type=MESH)
                told.append(True)
            focus(o, more[0])
            retire()
            if (o, more[0]) == (GROUPS - 1, 1):
                give(1, 0, partner)
                pl.semaphore_wait(ready, 1)
                give(1, 3, (hp + 1, t), hp < NH - 1)
                give(1, 4, (hp - 1, t), hp > 0)
    give(0, 1, (h + 1, t), h < NH - 1)
    give(0, 2, (h - 1, t), h > 0)

    def take(slot):
        got(vol_in.at[slot], ("volume", slot))

    @pl.when(h > 0)
    def _():
        take(3)
        take(1)

    @pl.when(h == 0)
    def _():
        vol_in[1] = jnp.zeros((8, 512), jnp.float32)
        vol_in[3] = jnp.zeros((8, 512), jnp.float32)

    @pl.when(h < NH - 1)
    def _():
        take(4)
        take(2)

    @pl.when(h == NH - 1)
    def _():
        vol_in[2] = jnp.zeros((8, 512), jnp.float32)
        vol_in[4] = jnp.zeros((8, 512), jnp.float32)

    take(0)
    here = vol[0] + vol_in[0]
    below = vol_in[1] + vol_in[3]
    above = vol_in[2] + vol_in[4]
    for part in range(2):
        rows = jnp.concatenate(
            [below[4 * part + 2 : 4 * part + 4], here[4 * part : 4 * part + 4], above[4 * part : 4 * part + 2]], axis=0
        )
        image = jnp.zeros((4, 512), jnp.float32)
        for j in range(5):
            image = image + taps_ref[j] * rows[j : j + 4]
        out_ref[part] = image * (1.0 / math.sqrt(8 * NH))

    retire()
    retire()


def local(pulse_panels, interp_weights, range_blocks, sector_of_panel, layer_cos, layer_sin, ground_cos, ground_sin, height_kernel):
    blocks = jnp.transpose(range_blocks[0], (2, 0, 1))
    f32, bf16, i32 = jnp.float32, jnp.bfloat16, jnp.int32
    ground = (2, 2, NZ, NY, 8, 512)
    return pl.pallas_call(
        kernel,
        out_shape=jax.ShapeDtypeStruct((2, 4, 512), f32),
        in_specs=[pl.BlockSpec(memory_space=pl.ANY)] * 9,
        out_specs=pl.BlockSpec(memory_space=pltpu.VMEM),
        scratch_shapes=[
            pltpu.VMEM((2, 8, WINDOW * 128), bf16),
            pltpu.VMEM((3, 4, 4), i32),
            pltpu.SMEM((3, 4, 4), i32),
            pltpu.SMEM((NH,), i32),
            pltpu.VMEM((4, 8, NH), f32),
            pltpu.VMEM((4, 8, NH), f32),
            pltpu.SMEM((5,), f32),
        ]
        + [pltpu.VMEM((BLOCKS, 2, 2, NY, 16, 128), bf16)] * GROUPS
        + [
            pltpu.VMEM((4, 4, 3, 128, 128), bf16),
            pltpu.VMEM((4, 4, 3, 128, 128), bf16),
            pltpu.VMEM((3, 4, 4), i32),
            pltpu.SMEM((3, 4, 4), i32),
            pltpu.VMEM((4, 8, NH), f32),
            pltpu.VMEM((4, 8, NH), f32),
            pltpu.VMEM((NZ, 2, NY, 8, 512), bf16),
            pltpu.VMEM((NZ, 2, NY, 8, 512), bf16),
            pltpu.VMEM((4, NZ, 2, NY, 16, 128), bf16),
            pltpu.VMEM((2, 16, HALF * 16), bf16),
            pltpu.VMEM((2, 8, 512), f32),
            pltpu.VMEM((5, 8, 512), f32),
            pltpu.SemaphoreType.DMA((N_SEND,)),
            pltpu.SemaphoreType.DMA((N_RECEIVE,)),
            pltpu.SemaphoreType.DMA((N_LOCAL + 1,)),
            pltpu.SemaphoreType.REGULAR,
        ],
        compiler_params=pltpu.CompilerParams(collective_id=0, has_side_effects=True, vmem_limit_bytes=62 << 20),
        name="focus",
    )(
        pulse_panels[0], interp_weights[0], blocks, sector_of_panel,
        jnp.swapaxes(layer_cos, 1, 2), jnp.swapaxes(layer_sin, 1, 2),
        ground_cos.reshape(ground), ground_sin.reshape(ground), height_kernel,
    )


def solution(mesh):
    in_specs = (
        P("height", None, None, "tile"),
        P("height", None, "tile", None, None, None),
        P("height", None, "tile", None),
        P(),
        P("height", None, None),
        P("height", None, None),
        P(None, None, "tile"),
        P(None, None, "tile"),
        P(),
    )
    return jax.shard_map(local, mesh=mesh, in_specs=in_specs, out_specs=P(None, "height", "tile"), check_vma=False)
```

```python
import math

import jax
import jax.numpy as jnp
from jax import lax
from jax.experimental import pallas as pl
from jax.experimental.pallas import tpu as pltpu
from jax.sharding import PartitionSpec as P

MESH = pl.DeviceIdType.MESH

NX, NZ, NY, NT = 4, 8, 4, 4
NH = NX * NZ * NY
HALF = NH // 2
WINDOW = 24
BLOCKS = WINDOW + 2
PART = 10
GROUPS = NZ // 2

A_MATE, B_Z, A_Z, B_DN, B_UP, B_FAR, A_DN, A_UP, ENDS, ENDS_MATE, ENDS_Z, COMPLETE, FOCUS = range(13)
ORDER = (
    (A_MATE, 0), (B_DN, 0), (B_UP, 0), (B_Z, 1), (ENDS, 0), (B_Z, 2), (A_DN, 0), (A_UP, 0), (B_FAR, 0), (B_Z, 4),
    (A_Z, 1), (B_DN, 1), (B_UP, 1), (B_DN, 2), (B_UP, 2), (A_Z, 2), (B_Z, 3), (B_DN, 4), (B_UP, 4), (B_Z, 5),
    (A_DN, 1), (A_UP, 1), (B_FAR, 1), (A_Z, 4), (B_Z, 6), (B_FAR, 2), (A_DN, 2), (A_UP, 2), (A_Z, 3), (B_DN, 3),
    (B_UP, 3), (B_FAR, 4), (B_DN, 5), (B_UP, 5), (A_Z, 5), (A_DN, 4), (A_UP, 4), (A_Z, 6), (B_Z, 7), (ENDS_MATE, 0),
    (B_DN, 6), (B_UP, 6), (A_DN, 3), (A_UP, 3), (B_FAR, 3), (B_FAR, 5), (A_DN, 5), (A_UP, 5), (A_Z, 7), (ENDS_Z, 0),
    (A_DN, 6), (A_UP, 6), (B_DN, 7), (B_UP, 7), (B_FAR, 6), (A_DN, 7), (A_UP, 7), (COMPLETE, 0), (COMPLETE, 1),
    (COMPLETE, 2), (B_FAR, 7), (FOCUS, 0, 0), (FOCUS, 0, 1), (FOCUS, 1, 0), (FOCUS, 1, 1), (COMPLETE, 3),
    (FOCUS, 2, 0), (FOCUS, 2, 1), (FOCUS, 3, 1), (FOCUS, 3, 0),
)
ONWARD = {0: (4, 2, 1), 4: (2, 1), 2: (1,), 6: (1,)}
N_SEND, N_RECEIVE, N_LOCAL = 256, 224, 24


def kernel(
    x_hbm, w_ref, blk_hbm, sector_hbm, cos_hbm, sin_hbm, gc_ref, gs_ref, taps_hbm, out_ref,
    x_ref, blk_v, blk_ref, sector_ref, cos_ref, sin_ref, taps_ref, data0, data1, data2, data3,
    w_own, w_far, blk_far, blk_smem, cos_far, sin_far, gcos, gsin, mask, rot, vol, vol_in,
    ssem, rsem, lsem, ready,
):
    data = (data0, data1, data2, data3)
    h, t = lax.axis_index("height"), lax.axis_index("tile")
    x, z, y = lax.div(h, NZ * NY), lax.rem(lax.div(h, NY), NZ), lax.rem(h, NY)
    half, xm = lax.div(x, 2), lax.rem(x, 2)

    def place(px, pz, py):
        return ((px * NZ + pz) * NY + py, t)

    def z_at(distance):
        flipped = z
        for bit in (1, 2, 4):
            if distance & bit:
                flipped = flipped + bit - 2 * bit * lax.rem(lax.div(z, bit), 2)
        return flipped

    y_up, y_dn, y_far = lax.rem(y + 1, NY), lax.rem(y + 3, NY), lax.rem(y + 2, NY)
    mate = place(x + 1 - 2 * xm, z, y)
    partner = place(3 - x, z, y)
    up, dn, opposite = place(x, z, y_up), place(x, z, y_dn), place(x, z, y_far)
    along = [place(x, z_at(d), y) for d in range(NZ)]
    hp = partner[0]

    receive_ids, sends = {}, []

    def receive_id(key):
        return receive_ids.setdefault(key, len(receive_ids))

    def edge(source, target, send_id, key, device):
        return pltpu.make_async_remote_copy(
            src_ref=source, dst_ref=target, send_sem=ssem.at[send_id], recv_sem=rsem.at[receive_id(key)],
            device_id=device, device_id_type=MESH,
        )

    def send(source, key, device, target=None, condition=None):
        number = len(sends)
        sends.append((source, condition))
        copy = edge(source, source if target is None else target, number, key, device)
        if condition is None:
            copy.start()
        else:
            pl.when(condition)(copy.start)

    def got(region, key):
        edge(region, region, 0, key, mate).wait_recv()

    retired = [0, 0]

    def retire():
        for number in range(*retired):
            source, condition = sends[number]
            copy = edge(source, source, number, ("a_mate", 0), mate)
            if condition is None:
                copy.wait_send()
            else:
                pl.when(condition)(copy.wait_send)
        retired[:] = [retired[1], len(sends)]

    def part_a(o, yi):
        return data[o // 2].at[pl.ds(0, PART), o % 2, :, yi]

    def half_a(m, o, yi):
        return data[o // 2].at[pl.ds(0, PART), o % 2, m, yi]

    def part_b(m, o, yi):
        return data[o // 2].at[pl.ds(PART, WINDOW - PART), o % 2, m, yi]

    def half_b(n, o, yi):
        middle = (WINDOW + PART) // 2
        start, stop = ((PART, middle), (middle, WINDOW))[n]
        return data[o // 2].at[pl.ds(start, stop - start), o % 2, xm, yi]

    core = lax.rem(t, 2)
    inner = lax.rem(t + 1, NT) >= 2
    far_block = WINDOW + lax.div(t, 2)

    def ends(o, yi):
        return data[o // 2].at[far_block, o % 2, :, yi]

    def ends_all(g, yi):
        return data[g].at[far_block, :, :, yi]

    def own(block):
        return data0.at[block, 0, xm, y]

    barrier = pltpu.get_barrier_semaphore()

    def greet(device):
        pl.semaphore_signal(barrier, inc=1, device_id=device, device_id_type=MESH)

    @pl.when(t > 0)
    def _():
        greet((h, t - 1))

    @pl.when(t < NT - 1)
    def _():
        greet((h, t + 1))

    near = [along[4], along[3], along[2], along[1], opposite, up, dn, mate, partner]
    for device in near:
        greet(device)

    local_copies = [
        (w_ref, w_own), (sector_hbm, sector_ref), (taps_hbm, taps_ref), (blk_hbm, blk_ref),
    ]
    for o in range(NZ):
        local_copies += [(gc_ref.at[half, :, z_at(o)], gcos.at[o]), (gs_ref.at[half, :, z_at(o)], gsin.at[o])]
    first_copies = [(x_hbm, x_ref), (blk_hbm, blk_v), (cos_hbm, cos_ref), (sin_hbm, sin_ref)]
    copies = [
        pltpu.make_async_copy(source, target, lsem.at[n]) for n, (source, target) in enumerate(first_copies + local_copies)
    ]
    for copy in copies:
        copy.start()
    for copy in copies[: len(first_copies)]:
        copy.wait()
    for b in range(WINDOW):
        lanes = slice(b * 128, (b + 1) * 128)
        data0[b, 0, xm, y] = jnp.concatenate([x_ref[0, :, lanes], x_ref[1, :, lanes]], axis=0)

    @pl.when(jnp.logical_not(inner))
    def _():
        for ref in data:
            ref[WINDOW + 1 - lax.div(t, 2)] = jnp.zeros((2, 2, NY, 16, 128), jnp.bfloat16)

    edges = len(near) + jnp.where(t > 0, 1, 0) + jnp.where(t < NT - 1, 1, 0)
    pl.semaphore_wait(barrier, edges)

    def spread_b(o):
        for d in ONWARD.get(o, ()):
            send(part_b(xm, o, y), ("bz", o ^ d), along[d], part_b(xm, o ^ d, y))
        send(part_b(xm, o, y), ("b_dn", o), up)
        send(part_b(xm, o, y), ("b_up", o), dn)
        send(part_b(xm, o, y), ("b_mate", o, 0), mate)

    def spread_a(o):
        for d in ONWARD.get(o, ()):
            send(part_a(o, y), ("az", o ^ d), along[d], part_a(o ^ d, y))
        send(part_a(o, y), ("a_dn", o), up)
        send(part_a(o, y), ("a_up", o), dn)

    send(half_a(xm, 0, y), ("a_mate", 0), mate)
    spread_b(0)
    send(own(WINDOW - 1), ("right",), (h, t + 1), own(WINDOW + 1), t == 1)
    send(own(0), ("left",), (h, t - 1), own(WINDOW), t == 2)
    send(cos_ref, ("cos",), partner, cos_far)
    send(sin_ref, ("sin",), partner, sin_far)
    send(blk_v, ("blocks",), partner, blk_far)
    for s in range(4):
        send(w_ref.at[s], ("weights", s), partner, w_far.at[s])

    def rotation(slab, cosine, sine):
        wide_shape = (NH, HALF * 16)
        column = lax.broadcasted_iota(jnp.int32, wide_shape, 1)
        row = lax.broadcasted_iota(jnp.int32, wide_shape, 0)
        z_of = lax.shift_right_logical(column, 7)
        z_of = jnp.bitwise_xor(z_of, jnp.full(wide_shape, z, jnp.int32))
        x_of = jnp.bitwise_and(lax.shift_right_logical(column, 6), 1) + 2 * half
        y_of = jnp.bitwise_and(lax.shift_right_logical(column, 4), 3)
        expand = ((x_of * NZ + z_of) * NY + y_of == row).astype(jnp.float32).astype(jnp.bfloat16)
        same = jnp.bitwise_and(column, 15) == jnp.bitwise_and(row, 15)
        rows = []
        for layer in range(4):
            rows += [cosine[layer], -sine[layer]]
        for layer in range(4):
            rows += [sine[layer], cosine[layer]]
        table = jnp.concatenate(rows, axis=0)
        high = table.astype(jnp.bfloat16)
        low = (table - high.astype(jnp.float32)).astype(jnp.bfloat16)
        halves = []
        for piece in (high, low):
            wide = jnp.dot(piece, expand, preferred_element_type=jnp.float32)
            wide = jnp.where(same, wide, 0.0)
            halves.append(jnp.sum(wide.reshape(8, 16, HALF * 16), axis=1))
        rot[slab] = jnp.concatenate(halves, axis=0).astype(jnp.bfloat16)

    rotation(0, cos_ref, sin_ref)
    for copy in copies[len(first_copies) :]:
        copy.wait()

    for o in range(NZ):

        @pl.loop(0, 2 * NY)
        def _(n):
            m, yi = lax.div(n, NY), lax.rem(n, NY)
            sector = sector_ref[((2 * half + m) * NZ + z_at(o)) * NY + yi]
            for s in range(4):
                one = jnp.where(sector == s, 1.0, 0.0).astype(jnp.float32)
                mask[s, o, m, yi] = jnp.full((16, 128), one, jnp.float32).astype(jnp.bfloat16)

    for slab in range(2):
        vol[slab] = jnp.zeros((8, 512), jnp.float32)

    def focus(g, slab):
        weights, blocks = ((w_own, blk_ref), (w_far, blk_smem))[slab]
        rotate = rot[slab, :, g * 256 : (g + 1) * 256]
        chosen = [mask[s, 2 * g : 2 * g + 2].reshape(16, 16, 128) for s in range(4)]
        for u in range(4):
            lanes = slice(u * 128, (u + 1) * 128)
            pieces = []
            for s in range(4):
                for k in range(3):
                    picked = data[g][lax.rem(blocks[k, s, u] + (BLOCKS - 1), BLOCKS)]
                    pieces.append((picked.reshape(16, 16, 128) * chosen[s]).reshape(256, 128))
            amplitude = jnp.dot(
                jnp.concatenate(pieces, axis=1), weights[:, u].reshape(12 * 128, 128),
                preferred_element_type=jnp.float32,
            ).reshape(16, 2, 8, 128)
            re, im = amplitude[:, 0], amplitude[:, 1]
            pc = gcos[2 * g : 2 * g + 2, :, :, :, lanes].reshape(16, 8, 128).astype(jnp.float32)
            ps = gsin[2 * g : 2 * g + 2, :, :, :, lanes].reshape(16, 8, 128).astype(jnp.float32)
            turned = jnp.concatenate([re * pc - im * ps, re * ps + im * pc], axis=1).reshape(256, 128)
            high = turned.astype(jnp.bfloat16)
            low = (turned - high.astype(jnp.float32)).astype(jnp.bfloat16)
            layers = jnp.dot(rotate, high, preferred_element_type=jnp.float32)
            layers = layers + jnp.dot(rotate, low, preferred_element_type=jnp.float32)
            vol[slab, :, lanes] += layers[:8] + layers[8:]

    complete, far_ready, told = set(), [], []

    def finish(g):
        for o in (2 * g, 2 * g + 1):
            for n, yi in enumerate((y, y_dn, y_up, y_far)):
                got(part_b(1 - xm, o, yi), ("b_mate", o, n))
            for m in range(2):
                got(half_a(m, o, y_far), ("a_far", m, o))

        @pl.when(inner)
        def _():
            for n, yi in enumerate((y_dn, y_up, y_far)):
                got(ends_all(g, yi), ("ends", n, g))

        send(data[g].at[(WINDOW - 1) * (1 - core)], ("core", g), (h, t + 1 - 2 * core), data[g].at[WINDOW + 1 - core])

    def weights_from_afar():
        if far_ready:
            return
        got(cos_far, ("cos",))
        got(sin_far, ("sin",))
        got(blk_far, ("blocks",))
        copy = pltpu.make_async_copy(blk_far, blk_smem, lsem.at[N_LOCAL - 1])
        copy.start()
        rotation(1, cos_far, sin_far)
        copy.wait()
        for s in range(4):
            got(w_far.at[s], ("weights", s))
        far_ready.append(True)

    def give(slab, slot, device, condition=None):
        send(vol.at[slab], ("volume", slot), device, vol_in.at[slot], condition)

    for what, o, *more in ORDER:
        if what == A_MATE:
            got(half_a(1 - xm, 0, y), ("a_mate", 0))
            spread_a(0)
        elif what == B_Z:
            got(part_b(xm, o, y), ("bz", o))
            spread_b(o)
        elif what == A_Z:
            got(part_a(o, y), ("az", o))
            spread_a(o)
        elif what == B_DN:
            got(part_b(xm, o, y_dn), ("b_dn", o))
            send(half_b(0, o, y_dn), ("b_far", 0, o), up)
            send(part_b(xm, o, y_dn), ("b_mate", o, 1), mate)
        elif what == B_UP:
            got(part_b(xm, o, y_up), ("b_up", o))
            send(half_b(1, o, y_up), ("b_far", 1, o), dn)
            send(part_b(xm, o, y_up), ("b_mate", o, 2), mate)
        elif what == B_FAR:
            for n in range(2):
                got(half_b(n, o, y_far), ("b_far", n, o))
            send(part_b(xm, o, y_far), ("b_mate", o, 3), mate)
        elif what == A_DN:
            got(part_a(o, y_dn), ("a_dn", o))
            send(half_a(0, o, y_dn), ("a_far", 0, o), up)
        elif what == A_UP:
            got(part_a(o, y_up), ("a_up", o))
            send(half_a(1, o, y_up), ("a_far", 1, o), dn)
        elif what == ENDS:
            pl.when(t == 2)(lambda: got(own(WINDOW + 1), ("right",)))
            pl.when(t == 1)(lambda: got(own(WINDOW), ("left",)))
            send(data0.at[far_block, 0, xm, y], ("ends_mate",), mate, condition=inner)
        elif what == ENDS_MATE:
            pl.when(inner)(lambda: got(data0.at[far_block, 0, 1 - xm, y], ("ends_mate",)))
            for d in range(NZ - 1, 0, -1):
                send(ends(0, y), ("ends_z", d), along[d], ends(d, y), inner)
        elif what == ENDS_Z:

            @pl.when(inner)
            def _():
                for d in range(1, NZ):
                    got(ends(d, y), ("ends_z", d))

            for g in range(GROUPS):
                for n, device in enumerate((up, dn, opposite)):
                    send(ends_all(g, y), ("ends", n, g), device, condition=inner)
        elif what == COMPLETE:
            finish(o)
        elif what == FOCUS:
            if o not in complete:
                complete.add(o)
                got(data[o].at[WINDOW + core], ("core", o))
            if more[0] == 1:
                weights_from_afar()
            if len(complete) == GROUPS and not told:
                pl.semaphore_signal(ready, inc=1, device_id=partner, device_id_type=MESH)
                told.append(True)
            focus(o, more[0])
            retire()
            if (o, more[0]) == (GROUPS - 1, 1):
                give(1, 0, partner)
                pl.semaphore_wait(ready, 1)
                give(1, 3, (hp + 1, t), hp < NH - 1)
                give(1, 4, (hp - 1, t), hp > 0)
    give(0, 1, (h + 1, t), h < NH - 1)
    give(0, 2, (h - 1, t), h > 0)

    def take(slot):
        got(vol_in.at[slot], ("volume", slot))

    @pl.when(h > 0)
    def _():
        take(3)
        take(1)

    @pl.when(h == 0)
    def _():
        vol_in[1] = jnp.zeros((8, 512), jnp.float32)
        vol_in[3] = jnp.zeros((8, 512), jnp.float32)

    @pl.when(h < NH - 1)
    def _():
        take(4)
        take(2)

    @pl.when(h == NH - 1)
    def _():
        vol_in[2] = jnp.zeros((8, 512), jnp.float32)
        vol_in[4] = jnp.zeros((8, 512), jnp.float32)

    take(0)
    here = vol[0] + vol_in[0]
    below = vol_in[1] + vol_in[3]
    above = vol_in[2] + vol_in[4]
    for part in range(2):
        rows = jnp.concatenate(
            [below[4 * part + 2 : 4 * part + 4], here[4 * part : 4 * part + 4], above[4 * part : 4 * part + 2]], axis=0
        )
        image = jnp.zeros((4, 512), jnp.float32)
        for j in range(5):
            image = image + taps_ref[j] * rows[j : j + 4]
        out_ref[part] = image * (1.0 / math.sqrt(8 * NH))

    retire()
    retire()


def local(pulse_panels, interp_weights, range_blocks, sector_of_panel, layer_cos, layer_sin, ground_cos, ground_sin, height_kernel):
    blocks = jnp.transpose(range_blocks[0], (2, 0, 1))
    f32, bf16, i32 = jnp.float32, jnp.bfloat16, jnp.int32
    ground = (2, 2, NZ, NY, 8, 512)
    return pl.pallas_call(
        kernel,
        out_shape=jax.ShapeDtypeStruct((2, 4, 512), f32),
        in_specs=[pl.BlockSpec(memory_space=pl.ANY)] * 9,
        out_specs=pl.BlockSpec(memory_space=pltpu.VMEM),
        scratch_shapes=[
            pltpu.VMEM((2, 8, WINDOW * 128), bf16),
            pltpu.VMEM((3, 4, 4), i32),
            pltpu.SMEM((3, 4, 4), i32),
            pltpu.SMEM((NH,), i32),
            pltpu.VMEM((4, 8, NH), f32),
            pltpu.VMEM((4, 8, NH), f32),
            pltpu.SMEM((5,), f32),
        ]
        + [pltpu.VMEM((BLOCKS, 2, 2, NY, 16, 128), bf16)] * GROUPS
        + [
            pltpu.VMEM((4, 4, 3, 128, 128), bf16),
            pltpu.VMEM((4, 4, 3, 128, 128), bf16),
            pltpu.VMEM((3, 4, 4), i32),
            pltpu.SMEM((3, 4, 4), i32),
            pltpu.VMEM((4, 8, NH), f32),
            pltpu.VMEM((4, 8, NH), f32),
            pltpu.VMEM((NZ, 2, NY, 8, 512), bf16),
            pltpu.VMEM((NZ, 2, NY, 8, 512), bf16),
            pltpu.VMEM((4, NZ, 2, NY, 16, 128), bf16),
            pltpu.VMEM((2, 16, HALF * 16), bf16),
            pltpu.VMEM((2, 8, 512), f32),
            pltpu.VMEM((5, 8, 512), f32),
            pltpu.SemaphoreType.DMA((N_SEND,)),
            pltpu.SemaphoreType.DMA((N_RECEIVE,)),
            pltpu.SemaphoreType.DMA((N_LOCAL + 1,)),
            pltpu.SemaphoreType.REGULAR,
        ],
        compiler_params=pltpu.CompilerParams(collective_id=0, has_side_effects=True, vmem_limit_bytes=62 << 20),
        name="focus",
    )(
        pulse_panels[0], interp_weights[0], blocks, sector_of_panel,
        jnp.swapaxes(layer_cos, 1, 2), jnp.swapaxes(layer_sin, 1, 2),
        ground_cos.reshape(ground), ground_sin.reshape(ground), height_kernel,
    )


def solution(mesh):
    in_specs = (
        P("height", None, None, "tile"),
        P("height", None, "tile", None, None, None),
        P("height", None, "tile", None),
        P(),
        P("height", None, None),
        P("height", None, None),
        P(None, None, "tile"),
        P(None, None, "tile"),
        P(),
    )
    return jax.shard_map(local, mesh=mesh, in_specs=in_specs, out_specs=P(None, "height", "tile"), check_vma=False)
```

```python
import math

import jax
import jax.numpy as jnp
from jax import lax
from jax.experimental import pallas as pl
from jax.experimental.pallas import tpu as pltpu
from jax.sharding import PartitionSpec as P

MESH = pl.DeviceIdType.MESH

NX, NZ, NY, NT = 4, 8, 4, 4
NH = NX * NZ * NY
HALF = NH // 2
WINDOW = 24
BLOCKS = WINDOW + 2
PART = 10
GROUPS = NZ // 2

A_MATE, B_Z, A_Z, B_DN, B_UP, B_FAR, A_DN, A_UP, ENDS, ENDS_MATE, ENDS_Z, ENDS_Y, COMPLETE, FOCUS = range(14)
ORDER = (
    (A_MATE, 0), (B_DN, 0), (B_UP, 0), (B_Z, 1), (B_Z, 2), (ENDS, 0), (A_DN, 0), (A_UP, 0), (B_FAR, 0), (A_Z, 1),
    (B_Z, 4), (B_DN, 1), (B_UP, 1), (B_DN, 2), (B_UP, 2), (A_Z, 2), (B_Z, 3), (ENDS_MATE, 0), (A_DN, 1), (A_UP, 1),
    (B_Z, 5), (ENDS_Z, 1), (B_DN, 4), (B_UP, 4), (ENDS_Z, 2), (B_FAR, 1), (B_Z, 6), (B_FAR, 2), (A_Z, 4),
    (ENDS_Z, 4), (A_Z, 3), (A_DN, 2), (A_UP, 2), (ENDS_Z, 3), (B_DN, 3), (B_UP, 3), (ENDS_Z, 5), (ENDS_Z, 6),
    (B_Z, 7), (B_DN, 5), (B_UP, 5), (B_FAR, 4), (B_DN, 6), (B_UP, 6), (ENDS_Z, 7), (ENDS_Y, 0), (A_Z, 5), (A_Z, 6),
    (A_DN, 4), (A_UP, 4), (A_DN, 3), (A_UP, 3), (B_FAR, 3), (B_DN, 7), (B_UP, 7), (A_Z, 7), (B_FAR, 5), (B_FAR, 6),
    (COMPLETE, 0), (A_DN, 5), (A_UP, 5), (FOCUS, 0, 0), (A_DN, 6), (A_UP, 6), (FOCUS, 0, 1), (B_FAR, 7),
    (COMPLETE, 1), (A_DN, 7), (A_UP, 7), (FOCUS, 1, 0), (FOCUS, 1, 1), (COMPLETE, 2), (FOCUS, 2, 0), (COMPLETE, 3),
    (FOCUS, 2, 1), (FOCUS, 3, 1), (FOCUS, 3, 0),
)
ONWARD = {0: (4, 2, 1), 4: (2, 1), 2: (1,), 6: (1,)}
IN_FLIGHT = 6
N_SEND, N_RECEIVE, N_LOCAL = 256, 224, 24


def kernel(
    x_hbm, w_ref, blk_hbm, sector_hbm, cos_hbm, sin_hbm, gc_ref, gs_ref, taps_hbm, out_ref,
    x_ref, blk_v, blk_ref, sector_ref, cos_ref, sin_ref, taps_ref, data0, data1, data2, data3,
    w_own, w_far, blk_far, blk_smem, cos_far, sin_far, gcos, gsin, sectors, rot, vol, vol_in,
    ssem, rsem, lsem, ready,
):
    data = (data0, data1, data2, data3)
    h, t = lax.axis_index("height"), lax.axis_index("tile")
    x, z, y = lax.div(h, NZ * NY), lax.rem(lax.div(h, NY), NZ), lax.rem(h, NY)
    half, xm = lax.div(x, 2), lax.rem(x, 2)

    def place(px, pz, py):
        return ((px * NZ + pz) * NY + py, t)

    def z_at(distance):
        flipped = z
        for bit in (1, 2, 4):
            if distance & bit:
                flipped = flipped + bit - 2 * bit * lax.rem(lax.div(z, bit), 2)
        return flipped

    def panel_at(o, m, yi):
        return ((2 * half + m) * NZ + z_at(o)) * NY + yi

    y_up, y_dn, y_far = lax.rem(y + 1, NY), lax.rem(y + 3, NY), lax.rem(y + 2, NY)
    mate = place(x + 1 - 2 * xm, z, y)
    partner = place(3 - x, z, y)
    up, dn, opposite = place(x, z, y_up), place(x, z, y_dn), place(x, z, y_far)
    along = [place(x, z_at(d), y) for d in range(NZ)]
    hp = partner[0]

    middle, edge_next, beside_edge = (
        jnp.logical_or(z == a, z == NZ - 1 - a) for a in (3, 2, 1)
    )
    inside = jnp.logical_or(edge_next, beside_edge)

    def onward(o):
        ways = [(d, beside_edge if (o, d) in ((2, 1), (6, 1)) else None) for d in ONWARD.get(o, ())]
        if o in (0, 4):
            ways += [(3, inside), (7, middle)]
        return ways

    receive_ids, sends, waited = {}, [], set()

    def receive_id(key):
        return receive_ids.setdefault(key, len(receive_ids))

    def edge(source, target, send_id, key, device):
        return pltpu.make_async_remote_copy(
            src_ref=source, dst_ref=target, send_sem=ssem.at[send_id], recv_sem=rsem.at[receive_id(key)],
            device_id=device, device_id_type=MESH,
        )

    def send(source, key, device, target=None, condition=None):
        number = len(sends)
        sends.append((source, condition))
        copy = edge(source, source if target is None else target, number, key, device)
        if condition is None:
            copy.start()
        else:
            pl.when(condition)(copy.start)

    to_mate = []

    def send_mate(source, key):
        to_mate.append(len(sends))
        if len(to_mate) > IN_FLIGHT:
            number = to_mate[-1 - IN_FLIGHT]
            if number not in waited:
                edge(sends[number][0], sends[number][0], number, key, mate).wait_send()
                waited.add(number)
        send(source, key, mate)

    def got(region, key):
        edge(region, region, 0, key, mate).wait_recv()

    retired = [0, 0]

    def retire():
        for number in range(*retired):
            source, condition = sends[number]
            if number in waited:
                continue
            waited.add(number)
            copy = edge(source, source, number, ("a_mate", 0), mate)
            if condition is None:
                copy.wait_send()
            else:
                pl.when(condition)(copy.wait_send)
        retired[:] = [retired[1], len(sends)]

    def part_a(o, yi):
        return data[o // 2].at[pl.ds(0, PART), o % 2, :, yi]

    def half_a(m, o, yi):
        return data[o // 2].at[pl.ds(0, PART), o % 2, m, yi]

    def part_b(m, o, yi):
        return data[o // 2].at[pl.ds(PART, WINDOW - PART), o % 2, m, yi]

    def half_b(n, o, yi):
        middle = (WINDOW + PART) // 2
        start, stop = ((PART, middle), (middle, WINDOW))[n]
        return data[o // 2].at[pl.ds(start, stop - start), o % 2, xm, yi]

    core = lax.rem(t, 2)
    inner = lax.rem(t + 1, NT) >= 2
    far_block = WINDOW + lax.div(t, 2)

    def ends(o, yi):
        return data[o // 2].at[far_block, o % 2, :, yi]

    def ends_all(g, yi):
        return data[g].at[far_block, :, :, yi]

    def own(block):
        return data0.at[block, 0, xm, y]

    barrier = pltpu.get_barrier_semaphore()

    def greet(device):
        pl.semaphore_signal(barrier, inc=1, device_id=device, device_id_type=MESH)

    @pl.when(t > 0)
    def _():
        greet((h, t - 1))

    @pl.when(t < NT - 1)
    def _():
        greet((h, t + 1))

    near = [along[4], along[2], along[1], opposite, up, dn, mate, partner]
    for device in near:
        greet(device)

    @pl.when(inside)
    def _():
        greet(along[3])

    @pl.when(middle)
    def _():
        greet(along[7])


    local_copies = [
        (w_ref, w_own), (sector_hbm, sector_ref), (taps_hbm, taps_ref), (blk_hbm, blk_ref),
    ]
    for o in range(NZ):
        local_copies += [(gc_ref.at[half, :, z_at(o)], gcos.at[o]), (gs_ref.at[half, :, z_at(o)], gsin.at[o])]
    first_copies = [(x_hbm, x_ref), (blk_hbm, blk_v), (cos_hbm, cos_ref), (sin_hbm, sin_ref)]
    copies = [
        pltpu.make_async_copy(source, target, lsem.at[n]) for n, (source, target) in enumerate(first_copies + local_copies)
    ]
    for copy in copies:
        copy.start()
    for copy in copies[: len(first_copies)]:
        copy.wait()
    for b in range(WINDOW):
        lanes = slice(b * 128, (b + 1) * 128)
        data0[b, 0, xm, y] = jnp.concatenate([x_ref[0, :, lanes], x_ref[1, :, lanes]], axis=0)

    @pl.when(jnp.logical_not(inner))
    def _():
        for ref in data:
            ref[WINDOW + 1 - lax.div(t, 2)] = jnp.zeros((2, 2, NY, 16, 128), jnp.bfloat16)

    edges = len(near) + jnp.where(t > 0, 1, 0) + jnp.where(t < NT - 1, 1, 0)
    edges = edges + jnp.where(jnp.logical_or(inside, middle), 1, 0)
    pl.semaphore_wait(barrier, edges)

    def spread_b(o):
        for d, condition in onward(o):
            send(part_b(xm, o, y), ("bz", o ^ d), along[d], part_b(xm, o ^ d, y), condition)
        send(part_b(xm, o, y), ("b_dn", o), up)
        send(part_b(xm, o, y), ("b_up", o), dn)
        send_mate(part_b(xm, o, y), ("b_mate", o, 0))

    def spread_a(o):
        for d, condition in onward(o):
            send(part_a(o, y), ("az", o ^ d), along[d], part_a(o ^ d, y), condition)
        send(part_a(o, y), ("a_dn", o), up)
        send(part_a(o, y), ("a_up", o), dn)

    def spread_ends(o):
        for d, condition in onward(o):
            both = inner if condition is None else jnp.logical_and(inner, condition)
            send(ends(o, y), ("ends_z", o ^ d), along[d], ends(o ^ d, y), both)

    send(half_a(xm, 0, y), ("a_mate", 0), mate)
    spread_b(0)
    send(own(WINDOW - 1), ("right",), (h, t + 1), own(WINDOW + 1), t == 1)
    send(own(0), ("left",), (h, t - 1), own(WINDOW), t == 2)
    send(cos_ref, ("cos",), partner, cos_far)
    send(sin_ref, ("sin",), partner, sin_far)
    send(blk_v, ("blocks",), partner, blk_far)
    for s in range(4):
        send(w_ref.at[s], ("weights", s), partner, w_far.at[s])

    def rotation(slab, cosine, sine):
        wide_shape = (NH, HALF * 16)
        column = lax.broadcasted_iota(jnp.int32, wide_shape, 1)
        row = lax.broadcasted_iota(jnp.int32, wide_shape, 0)
        z_of = lax.shift_right_logical(column, 7)
        z_of = jnp.bitwise_xor(z_of, jnp.full(wide_shape, z, jnp.int32))
        x_of = jnp.bitwise_and(lax.shift_right_logical(column, 6), 1) + 2 * half
        y_of = jnp.bitwise_and(lax.shift_right_logical(column, 4), 3)
        expand = ((x_of * NZ + z_of) * NY + y_of == row).astype(jnp.float32).astype(jnp.bfloat16)
        same = jnp.bitwise_and(column, 15) == jnp.bitwise_and(row, 15)
        rows = []
        for layer in range(4):
            rows += [cosine[layer], -sine[layer]]
        for layer in range(4):
            rows += [sine[layer], cosine[layer]]
        table = jnp.concatenate(rows, axis=0)
        high = table.astype(jnp.bfloat16)
        low = (table - high.astype(jnp.float32)).astype(jnp.bfloat16)
        halves = []
        for piece in (high, low):
            wide = jnp.dot(piece, expand, preferred_element_type=jnp.float32)
            wide = jnp.where(same, wide, 0.0)
            halves.append(jnp.sum(wide.reshape(8, 16, HALF * 16), axis=1))
        rot[slab] = jnp.concatenate(halves, axis=0).astype(jnp.bfloat16)

    rotation(0, cos_ref, sin_ref)
    for copy in copies[len(first_copies) :]:
        copy.wait()

    for o in range(NZ):

        @pl.loop(0, 2 * NY)
        def _(n):
            m, yi = lax.div(n, NY), lax.rem(n, NY)
            sectors[o, m, yi] = jnp.full((16, 128), sector_ref[panel_at(o, m, yi)], jnp.int32)

    for slab in range(2):
        vol[slab] = jnp.zeros((8, 512), jnp.float32)

    def focus(g, slab):
        weights, blocks = ((w_own, blk_ref), (w_far, blk_smem))[slab]
        rotate = rot[slab, :, g * 256 : (g + 1) * 256]
        of_rows = sectors[2 * g : 2 * g + 2].reshape(256, 128)
        places = [(n, m, yi) for n in range(2) for m in range(2) for yi in range(NY)]
        chosen = [sector_ref[panel_at(2 * g + n, m, yi)] for n, m, yi in places]
        highs, lows = [], []
        for u in range(4):
            lanes = slice(u * 128, (u + 1) * 128)
            columns = []
            for k in range(3):
                rows = []
                for (n, m, yi), s in zip(places, chosen):
                    rows.append(data[g][lax.rem(blocks[k, s, u] + (BLOCKS - 1), BLOCKS), n, m, yi])
                columns.append(jnp.concatenate(rows, axis=0))
            every = jnp.dot(
                jnp.concatenate(columns, axis=1),
                jnp.concatenate([weights[s, u].reshape(3 * 128, 128) for s in range(4)], axis=1),
                preferred_element_type=jnp.float32,
            )
            amplitude = every[:, 3 * 128 :]
            for s in range(3):
                amplitude = jnp.where(of_rows == s, every[:, s * 128 : (s + 1) * 128], amplitude)
            amplitude = amplitude.reshape(16, 2, 8, 128)
            re, im = amplitude[:, 0], amplitude[:, 1]
            pc = gcos[2 * g : 2 * g + 2, :, :, :, lanes].reshape(16, 8, 128).astype(jnp.float32)
            ps = gsin[2 * g : 2 * g + 2, :, :, :, lanes].reshape(16, 8, 128).astype(jnp.float32)
            turned = jnp.concatenate([re * pc - im * ps, re * ps + im * pc], axis=1).reshape(256, 128)
            high = turned.astype(jnp.bfloat16)
            highs.append(high)
            lows.append((turned - high.astype(jnp.float32)).astype(jnp.bfloat16))
        layers = jnp.dot(rotate, jnp.concatenate(highs, axis=1), preferred_element_type=jnp.float32)
        layers = layers + jnp.dot(rotate, jnp.concatenate(lows, axis=1), preferred_element_type=jnp.float32)
        vol[slab] += layers[:8] + layers[8:]

    complete, far_ready, told = set(), [], []

    def finish(g):
        for o in (2 * g, 2 * g + 1):
            for n, yi in enumerate((y, y_dn, y_up, y_far)):
                got(part_b(1 - xm, o, yi), ("b_mate", o, n))
            for m in range(2):
                got(half_a(m, o, y_far), ("a_far", m, o))

        @pl.when(inner)
        def _():
            for n, yi in enumerate((y_dn, y_up, y_far)):
                got(ends_all(g, yi), ("ends", n, g))

        send(data[g].at[(WINDOW - 1) * (1 - core)], ("core", g), (h, t + 1 - 2 * core), data[g].at[WINDOW + 1 - core])

    def weights_from_afar():
        if far_ready:
            return
        got(cos_far, ("cos",))
        got(sin_far, ("sin",))
        got(blk_far, ("blocks",))
        copy = pltpu.make_async_copy(blk_far, blk_smem, lsem.at[N_LOCAL - 1])
        copy.start()
        rotation(1, cos_far, sin_far)
        copy.wait()
        for s in range(4):
            got(w_far.at[s], ("weights", s))
        far_ready.append(True)

    def give(slab, slot, device, condition=None):
        send(vol.at[slab], ("volume", slot), device, vol_in.at[slot], condition)

    for what, o, *more in ORDER:
        if what == A_MATE:
            got(half_a(1 - xm, 0, y), ("a_mate", 0))
            spread_a(0)
        elif what == B_Z:
            got(part_b(xm, o, y), ("bz", o))
            spread_b(o)
        elif what == A_Z:
            got(part_a(o, y), ("az", o))
            spread_a(o)
        elif what == B_DN:
            got(part_b(xm, o, y_dn), ("b_dn", o))
            send(half_b(0, o, y_dn), ("b_far", 0, o), up)
            send_mate(part_b(xm, o, y_dn), ("b_mate", o, 1))
        elif what == B_UP:
            got(part_b(xm, o, y_up), ("b_up", o))
            send(half_b(1, o, y_up), ("b_far", 1, o), dn)
            send_mate(part_b(xm, o, y_up), ("b_mate", o, 2))
        elif what == B_FAR:
            for n in range(2):
                got(half_b(n, o, y_far), ("b_far", n, o))
            send_mate(part_b(xm, o, y_far), ("b_mate", o, 3))
        elif what == A_DN:
            got(part_a(o, y_dn), ("a_dn", o))
            send(half_a(0, o, y_dn), ("a_far", 0, o), up)
        elif what == A_UP:
            got(part_a(o, y_up), ("a_up", o))
            send(half_a(1, o, y_up), ("a_far", 1, o), dn)
        elif what == ENDS:
            pl.when(t == 2)(lambda: got(own(WINDOW + 1), ("right",)))
            pl.when(t == 1)(lambda: got(own(WINDOW), ("left",)))
            send(data0.at[far_block, 0, xm, y], ("ends_mate",), mate, condition=inner)
        elif what == ENDS_MATE:
            pl.when(inner)(lambda: got(data0.at[far_block, 0, 1 - xm, y], ("ends_mate",)))
            spread_ends(0)
        elif what == ENDS_Z:
            pl.when(inner)(lambda: got(ends(o, y), ("ends_z", o)))
            spread_ends(o)
        elif what == ENDS_Y:
            for g in range(GROUPS):
                for n, device in enumerate((up, dn, opposite)):
                    send(ends_all(g, y), ("ends", n, g), device, condition=inner)
        elif what == COMPLETE:
            finish(o)
        elif what == FOCUS:
            if o not in complete:
                complete.add(o)
                got(data[o].at[WINDOW + core], ("core", o))
            if more[0] == 1:
                weights_from_afar()
            if len(complete) == GROUPS and not told:
                pl.semaphore_signal(ready, inc=1, device_id=partner, device_id_type=MESH)
                told.append(True)
            focus(o, more[0])
            if o < GROUPS - 1:
                retire()
            if (o, more[0]) == (GROUPS - 1, 1):
                give(1, 0, partner)
                pl.semaphore_wait(ready, 1)
                give(1, 3, (hp + 1, t), hp < NH - 1)
                give(1, 4, (hp - 1, t), hp > 0)
    give(0, 1, (h + 1, t), h < NH - 1)
    give(0, 2, (h - 1, t), h > 0)

    def take(slot):
        got(vol_in.at[slot], ("volume", slot))

    @pl.when(h > 0)
    def _():
        take(3)
        take(1)

    @pl.when(h == 0)
    def _():
        vol_in[1] = jnp.zeros((8, 512), jnp.float32)
        vol_in[3] = jnp.zeros((8, 512), jnp.float32)

    @pl.when(h < NH - 1)
    def _():
        take(4)
        take(2)

    @pl.when(h == NH - 1)
    def _():
        vol_in[2] = jnp.zeros((8, 512), jnp.float32)
        vol_in[4] = jnp.zeros((8, 512), jnp.float32)

    take(0)
    here = vol[0] + vol_in[0]
    below = vol_in[1] + vol_in[3]
    above = vol_in[2] + vol_in[4]
    for part in range(2):
        rows = jnp.concatenate(
            [below[4 * part + 2 : 4 * part + 4], here[4 * part : 4 * part + 4], above[4 * part : 4 * part + 2]], axis=0
        )
        image = jnp.zeros((4, 512), jnp.float32)
        for j in range(5):
            image = image + taps_ref[j] * rows[j : j + 4]
        out_ref[part] = image * (1.0 / math.sqrt(8 * NH))

    retire()
    retire()


def local(pulse_panels, interp_weights, range_blocks, sector_of_panel, layer_cos, layer_sin, ground_cos, ground_sin, height_kernel):
    blocks = jnp.transpose(range_blocks[0], (2, 0, 1))
    f32, bf16, i32 = jnp.float32, jnp.bfloat16, jnp.int32
    ground = (2, 2, NZ, NY, 8, 512)
    return pl.pallas_call(
        kernel,
        out_shape=jax.ShapeDtypeStruct((2, 4, 512), f32),
        in_specs=[pl.BlockSpec(memory_space=pl.ANY)] * 9,
        out_specs=pl.BlockSpec(memory_space=pltpu.VMEM),
        scratch_shapes=[
            pltpu.VMEM((2, 8, WINDOW * 128), bf16),
            pltpu.VMEM((3, 4, 4), i32),
            pltpu.SMEM((3, 4, 4), i32),
            pltpu.SMEM((NH,), i32),
            pltpu.VMEM((4, 8, NH), f32),
            pltpu.VMEM((4, 8, NH), f32),
            pltpu.SMEM((5,), f32),
        ]
        + [pltpu.VMEM((BLOCKS, 2, 2, NY, 16, 128), bf16)] * GROUPS
        + [
            pltpu.VMEM((4, 4, 3, 128, 128), bf16),
            pltpu.VMEM((4, 4, 3, 128, 128), bf16),
            pltpu.VMEM((3, 4, 4), i32),
            pltpu.SMEM((3, 4, 4), i32),
            pltpu.VMEM((4, 8, NH), f32),
            pltpu.VMEM((4, 8, NH), f32),
            pltpu.VMEM((NZ, 2, NY, 8, 512), bf16),
            pltpu.VMEM((NZ, 2, NY, 8, 512), bf16),
            pltpu.VMEM((NZ, 2, NY, 16, 128), i32),
            pltpu.VMEM((2, 16, HALF * 16), bf16),
            pltpu.VMEM((2, 8, 512), f32),
            pltpu.VMEM((5, 8, 512), f32),
            pltpu.SemaphoreType.DMA((N_SEND,)),
            pltpu.SemaphoreType.DMA((N_RECEIVE,)),
            pltpu.SemaphoreType.DMA((N_LOCAL + 1,)),
            pltpu.SemaphoreType.REGULAR,
        ],
        compiler_params=pltpu.CompilerParams(collective_id=0, has_side_effects=True, vmem_limit_bytes=62 << 20),
        name="focus",
    )(
        pulse_panels[0], interp_weights[0], blocks, sector_of_panel,
        jnp.swapaxes(layer_cos, 1, 2), jnp.swapaxes(layer_sin, 1, 2),
        ground_cos.reshape(ground), ground_sin.reshape(ground), height_kernel,
    )


def solution(mesh):
    in_specs = (
        P("height", None, None, "tile"),
        P("height", None, "tile", None, None, None),
        P("height", None, "tile", None),
        P(),
        P("height", None, None),
        P("height", None, None),
        P(None, None, "tile"),
        P(None, None, "tile"),
        P(),
    )
    return jax.shard_map(local, mesh=mesh, in_specs=in_specs, out_specs=P(None, "height", "tile"), check_vma=False)
```

```python
import math

import jax
import jax.numpy as jnp
from jax import lax
from jax.experimental import pallas as pl
from jax.experimental.pallas import tpu as pltpu
from jax.sharding import PartitionSpec as P

MESH = pl.DeviceIdType.MESH

NX, NZ, NY, NT = 4, 8, 4, 4
NH = NX * NZ * NY
HALF = NH // 2
WINDOW = 24
BLOCKS = WINDOW + 2
PART = 10
GROUPS = NZ // 2

A_MATE, B_Z, A_Z, B_DN, B_UP, B_FAR, A_DN, A_UP, ENDS, ENDS_MATE, ENDS_Z, ENDS_Y, COMPLETE, FOCUS = range(14)
ORDER = (
    (A_MATE, 0), (B_DN, 0), (B_UP, 0), (B_Z, 1), (B_Z, 2), (ENDS, 0), (A_DN, 0), (A_UP, 0), (B_FAR, 0), (A_Z, 1),
    (B_Z, 4), (B_DN, 1), (B_UP, 1), (B_DN, 2), (B_UP, 2), (A_Z, 2), (B_Z, 3), (ENDS_MATE, 0), (A_DN, 1), (A_UP, 1),
    (B_Z, 5), (ENDS_Z, 1), (B_DN, 4), (B_UP, 4), (ENDS_Z, 2), (B_FAR, 1), (B_Z, 6), (B_FAR, 2), (A_Z, 4),
    (ENDS_Z, 4), (A_Z, 3), (A_DN, 2), (A_UP, 2), (ENDS_Z, 3), (B_DN, 3), (B_UP, 3), (ENDS_Z, 5), (ENDS_Z, 6),
    (B_Z, 7), (B_DN, 5), (B_UP, 5), (B_FAR, 4), (B_DN, 6), (B_UP, 6), (ENDS_Z, 7), (ENDS_Y, 0), (A_Z, 5), (A_Z, 6),
    (A_DN, 4), (A_UP, 4), (A_DN, 3), (A_UP, 3), (B_FAR, 3), (B_DN, 7), (B_UP, 7), (A_Z, 7), (B_FAR, 5), (B_FAR, 6),
    (COMPLETE, 0), (A_DN, 5), (A_UP, 5), (FOCUS, 0, 0), (A_DN, 6), (A_UP, 6), (FOCUS, 0, 1), (B_FAR, 7),
    (COMPLETE, 1), (A_DN, 7), (A_UP, 7), (FOCUS, 1, 0), (FOCUS, 1, 1), (COMPLETE, 2), (FOCUS, 2, 0), (COMPLETE, 3),
    (FOCUS, 2, 1), (FOCUS, 3, 1), (FOCUS, 3, 0),
)
ONWARD = {0: (4, 2, 1), 4: (2, 1), 2: (1,), 6: (1,)}
IN_FLIGHT = 6
N_SEND, N_RECEIVE, N_LOCAL = 256, 224, 24


def kernel(
    x_hbm, w_ref, blk_hbm, sector_hbm, cos_hbm, sin_hbm, gc_ref, gs_ref, taps_hbm, out_ref,
    x_ref, blk_v, blk_ref, sector_ref, cos_ref, sin_ref, taps_ref, data0, data1, data2, data3,
    w_own, w_far, blk_far, blk_smem, cos_far, sin_far, gcos, gsin, sectors, rot, vol, vol_in,
    ssem, rsem, lsem, ready,
):
    data = (data0, data1, data2, data3)
    h, t = lax.axis_index("height"), lax.axis_index("tile")
    x, z, y = lax.div(h, NZ * NY), lax.rem(lax.div(h, NY), NZ), lax.rem(h, NY)
    half, xm = lax.div(x, 2), lax.rem(x, 2)

    def place(px, pz, py):
        return ((px * NZ + pz) * NY + py, t)

    def z_at(distance):
        flipped = z
        for bit in (1, 2, 4):
            if distance & bit:
                flipped = flipped + bit - 2 * bit * lax.rem(lax.div(z, bit), 2)
        return flipped

    def panel_at(o, m, yi):
        return ((2 * half + m) * NZ + z_at(o)) * NY + yi

    y_up, y_dn, y_far = lax.rem(y + 1, NY), lax.rem(y + 3, NY), lax.rem(y + 2, NY)
    mate = place(x + 1 - 2 * xm, z, y)
    partner = place(3 - x, z, y)
    up, dn, opposite = place(x, z, y_up), place(x, z, y_dn), place(x, z, y_far)
    along = [place(x, z_at(d), y) for d in range(NZ)]
    hp = partner[0]

    middle, edge_next, beside_edge = (
        jnp.logical_or(z == a, z == NZ - 1 - a) for a in (3, 2, 1)
    )
    inside = jnp.logical_or(edge_next, beside_edge)

    def onward(o):
        ways = [(d, beside_edge if (o, d) in ((2, 1), (6, 1)) else None) for d in ONWARD.get(o, ())]
        if o in (0, 4):
            ways += [(3, inside), (7, middle)]
        return ways

    receive_ids, sends, waited = {}, [], set()

    def receive_id(key):
        return receive_ids.setdefault(key, len(receive_ids))

    def edge(source, target, send_id, key, device):
        return pltpu.make_async_remote_copy(
            src_ref=source, dst_ref=target, send_sem=ssem.at[send_id], recv_sem=rsem.at[receive_id(key)],
            device_id=device, device_id_type=MESH,
        )

    def send(source, key, device, target=None, condition=None):
        number = len(sends)
        sends.append((source, condition))
        copy = edge(source, source if target is None else target, number, key, device)
        if condition is None:
            copy.start()
        else:
            pl.when(condition)(copy.start)

    to_mate = []

    def send_mate(source, key):
        to_mate.append(len(sends))
        if len(to_mate) > IN_FLIGHT:
            number = to_mate[-1 - IN_FLIGHT]
            if number not in waited:
                edge(sends[number][0], sends[number][0], number, key, mate).wait_send()
                waited.add(number)
        send(source, key, mate)

    def got(region, key):
        edge(region, region, 0, key, mate).wait_recv()

    retired = [0, 0]

    def retire():
        for number in range(*retired):
            source, condition = sends[number]
            if number in waited:
                continue
            waited.add(number)
            copy = edge(source, source, number, ("a_mate", 0), mate)
            if condition is None:
                copy.wait_send()
            else:
                pl.when(condition)(copy.wait_send)
        retired[:] = [retired[1], len(sends)]

    def part_a(o, yi):
        return data[o // 2].at[pl.ds(0, PART), o % 2, :, yi]

    def half_a(m, o, yi):
        return data[o // 2].at[pl.ds(0, PART), o % 2, m, yi]

    def part_b(m, o, yi):
        return data[o // 2].at[pl.ds(PART, WINDOW - PART), o % 2, m, yi]

    def half_b(n, o, yi):
        middle = (WINDOW + PART) // 2
        start, stop = ((PART, middle), (middle, WINDOW))[n]
        return data[o // 2].at[pl.ds(start, stop - start), o % 2, xm, yi]

    core = lax.rem(t, 2)
    inner = lax.rem(t + 1, NT) >= 2
    far_block = WINDOW + lax.div(t, 2)

    def ends(o, yi):
        return data[o // 2].at[far_block, o % 2, :, yi]

    def ends_all(g, yi):
        return data[g].at[far_block, :, :, yi]

    def own(block):
        return data0.at[block, 0, xm, y]

    barrier = pltpu.get_barrier_semaphore()

    def greet(device):
        pl.semaphore_signal(barrier, inc=1, device_id=device, device_id_type=MESH)

    @pl.when(t > 0)
    def _():
        greet((h, t - 1))

    @pl.when(t < NT - 1)
    def _():
        greet((h, t + 1))

    near = [along[4], along[2], along[1], opposite, up, dn, mate, partner]
    for device in near:
        greet(device)

    @pl.when(inside)
    def _():
        greet(along[3])

    @pl.when(middle)
    def _():
        greet(along[7])


    local_copies = [
        (w_ref, w_own), (sector_hbm, sector_ref), (taps_hbm, taps_ref), (blk_hbm, blk_ref),
    ]
    for o in range(NZ):
        local_copies += [(gc_ref.at[half, :, z_at(o)], gcos.at[o]), (gs_ref.at[half, :, z_at(o)], gsin.at[o])]
    first_copies = [(x_hbm, x_ref), (blk_hbm, blk_v), (cos_hbm, cos_ref), (sin_hbm, sin_ref)]
    copies = [
        pltpu.make_async_copy(source, target, lsem.at[n]) for n, (source, target) in enumerate(first_copies + local_copies)
    ]
    for copy in copies:
        copy.start()
    for copy in copies[: len(first_copies)]:
        copy.wait()
    for b in range(WINDOW):
        lanes = slice(b * 128, (b + 1) * 128)
        data0[b, 0, xm, y] = jnp.concatenate([x_ref[0, :, lanes], x_ref[1, :, lanes]], axis=0)

    @pl.when(jnp.logical_not(inner))
    def _():
        for ref in data:
            ref[WINDOW + 1 - lax.div(t, 2)] = jnp.zeros((2, 2, NY, 16, 128), jnp.bfloat16)

    edges = len(near) + jnp.where(t > 0, 1, 0) + jnp.where(t < NT - 1, 1, 0)
    edges = edges + jnp.where(jnp.logical_or(inside, middle), 1, 0)
    pl.semaphore_wait(barrier, edges)

    def spread_b(o):
        for d, condition in onward(o):
            send(part_b(xm, o, y), ("bz", o ^ d), along[d], part_b(xm, o ^ d, y), condition)
        send(part_b(xm, o, y), ("b_dn", o), up)
        send(part_b(xm, o, y), ("b_up", o), dn)
        send_mate(part_b(xm, o, y), ("b_mate", o, 0))

    def spread_a(o):
        for d, condition in onward(o):
            send(part_a(o, y), ("az", o ^ d), along[d], part_a(o ^ d, y), condition)
        send(part_a(o, y), ("a_dn", o), up)
        send(part_a(o, y), ("a_up", o), dn)

    def spread_ends(o):
        for d, condition in onward(o):
            both = inner if condition is None else jnp.logical_and(inner, condition)
            send(ends(o, y), ("ends_z", o ^ d), along[d], ends(o ^ d, y), both)

    send(half_a(xm, 0, y), ("a_mate", 0), mate)
    spread_b(0)
    send(own(WINDOW - 1), ("right",), (h, t + 1), own(WINDOW + 1), t == 1)
    send(own(0), ("left",), (h, t - 1), own(WINDOW), t == 2)
    send(cos_ref, ("cos",), partner, cos_far)
    send(sin_ref, ("sin",), partner, sin_far)
    send(blk_v, ("blocks",), partner, blk_far)
    for s in range(4):
        send(w_ref.at[s], ("weights", s), partner, w_far.at[s])

    def rotation(slab, cosine, sine):
        wide_shape = (NH, HALF * 16)
        column = lax.broadcasted_iota(jnp.int32, wide_shape, 1)
        row = lax.broadcasted_iota(jnp.int32, wide_shape, 0)
        z_of = lax.shift_right_logical(column, 7)
        z_of = jnp.bitwise_xor(z_of, jnp.full(wide_shape, z, jnp.int32))
        x_of = jnp.bitwise_and(lax.shift_right_logical(column, 6), 1) + 2 * half
        y_of = jnp.bitwise_and(lax.shift_right_logical(column, 4), 3)
        expand = ((x_of * NZ + z_of) * NY + y_of == row).astype(jnp.float32).astype(jnp.bfloat16)
        same = jnp.bitwise_and(column, 15) == jnp.bitwise_and(row, 15)
        rows = []
        for layer in range(4):
            rows += [cosine[layer], -sine[layer]]
        for layer in range(4):
            rows += [sine[layer], cosine[layer]]
        table = jnp.concatenate(rows, axis=0)
        high = table.astype(jnp.bfloat16)
        low = (table - high.astype(jnp.float32)).astype(jnp.bfloat16)
        halves = []
        for piece in (high, low):
            wide = jnp.dot(piece, expand, preferred_element_type=jnp.float32)
            wide = jnp.where(same, wide, 0.0)
            halves.append(jnp.sum(wide.reshape(8, 16, HALF * 16), axis=1))
        rot[slab] = jnp.concatenate(halves, axis=0).astype(jnp.bfloat16)

    rotation(0, cos_ref, sin_ref)
    for copy in copies[len(first_copies) :]:
        copy.wait()

    for o in range(NZ):

        @pl.loop(0, 2 * NY)
        def _(n):
            m, yi = lax.div(n, NY), lax.rem(n, NY)
            sectors[o, m, yi] = jnp.full((16, 128), sector_ref[panel_at(o, m, yi)], jnp.int32)

    for slab in range(2):
        vol[slab] = jnp.zeros((8, 512), jnp.float32)

    def focus(g, slab):
        weights, blocks = ((w_own, blk_ref), (w_far, blk_smem))[slab]
        rotate = rot[slab, :, g * 256 : (g + 1) * 256]
        of_rows = sectors[2 * g : 2 * g + 2].reshape(256, 128)
        places = [(n, m, yi) for n in range(2) for m in range(2) for yi in range(NY)]
        chosen = [sector_ref[panel_at(2 * g + n, m, yi)] for n, m, yi in places]
        highs, lows = [], []
        for u in range(4):
            lanes = slice(u * 128, (u + 1) * 128)
            columns = []
            for k in range(3):
                rows = []
                for (n, m, yi), s in zip(places, chosen):
                    rows.append(data[g][lax.rem(blocks[k, s, u] + (BLOCKS - 1), BLOCKS), n, m, yi])
                columns.append(jnp.concatenate(rows, axis=0))
            every = jnp.dot(
                jnp.concatenate(columns, axis=1),
                jnp.concatenate([weights[s, u].reshape(3 * 128, 128) for s in range(4)], axis=1),
                preferred_element_type=jnp.float32,
            )
            amplitude = every[:, 3 * 128 :]
            for s in range(3):
                amplitude = jnp.where(of_rows == s, every[:, s * 128 : (s + 1) * 128], amplitude)
            amplitude = amplitude.reshape(16, 2, 8, 128)
            re, im = amplitude[:, 0], amplitude[:, 1]
            pc = gcos[2 * g : 2 * g + 2, :, :, :, lanes].reshape(16, 8, 128).astype(jnp.float32)
            ps = gsin[2 * g : 2 * g + 2, :, :, :, lanes].reshape(16, 8, 128).astype(jnp.float32)
            turned = jnp.concatenate([re * pc - im * ps, re * ps + im * pc], axis=1).reshape(256, 128)
            high = turned.astype(jnp.bfloat16)
            highs.append(high)
            lows.append((turned - high.astype(jnp.float32)).astype(jnp.bfloat16))
        layers = jnp.dot(rotate, jnp.concatenate(highs, axis=1), preferred_element_type=jnp.float32)
        layers = layers + jnp.dot(rotate, jnp.concatenate(lows, axis=1), preferred_element_type=jnp.float32)
        vol[slab] += layers[:8] + layers[8:]

    complete, far_ready, told = set(), [], []

    def finish(g):
        for o in (2 * g, 2 * g + 1):
            for n, yi in enumerate((y, y_dn, y_up, y_far)):
                got(part_b(1 - xm, o, yi), ("b_mate", o, n))
            for m in range(2):
                got(half_a(m, o, y_far), ("a_far", m, o))

        @pl.when(inner)
        def _():
            for n, yi in enumerate((y_dn, y_up, y_far)):
                got(ends_all(g, yi), ("ends", n, g))

        send(data[g].at[(WINDOW - 1) * (1 - core)], ("core", g), (h, t + 1 - 2 * core), data[g].at[WINDOW + 1 - core])

    def tables_from_afar():
        got(cos_far, ("cos",))
        got(sin_far, ("sin",))
        got(blk_far, ("blocks",))
        copy = pltpu.make_async_copy(blk_far, blk_smem, lsem.at[N_LOCAL - 1])
        copy.start()
        rotation(1, cos_far, sin_far)
        copy.wait()

    def weights_from_afar():
        if far_ready:
            return
        for s in range(4):
            got(w_far.at[s], ("weights", s))
        far_ready.append(True)

    def give(slab, slot, device, condition=None):
        send(vol.at[slab], ("volume", slot), device, vol_in.at[slot], condition)

    for what, o, *more in ORDER:
        if what == A_MATE:
            got(half_a(1 - xm, 0, y), ("a_mate", 0))
            spread_a(0)
        elif what == B_Z:
            got(part_b(xm, o, y), ("bz", o))
            spread_b(o)
        elif what == A_Z:
            got(part_a(o, y), ("az", o))
            spread_a(o)
        elif what == B_DN:
            got(part_b(xm, o, y_dn), ("b_dn", o))
            send(half_b(0, o, y_dn), ("b_far", 0, o), up)
            send_mate(part_b(xm, o, y_dn), ("b_mate", o, 1))
        elif what == B_UP:
            got(part_b(xm, o, y_up), ("b_up", o))
            send(half_b(1, o, y_up), ("b_far", 1, o), dn)
            send_mate(part_b(xm, o, y_up), ("b_mate", o, 2))
        elif what == B_FAR:
            for n in range(2):
                got(half_b(n, o, y_far), ("b_far", n, o))
            send_mate(part_b(xm, o, y_far), ("b_mate", o, 3))
        elif what == A_DN:
            got(part_a(o, y_dn), ("a_dn", o))
            send(half_a(0, o, y_dn), ("a_far", 0, o), up)
        elif what == A_UP:
            got(part_a(o, y_up), ("a_up", o))
            send(half_a(1, o, y_up), ("a_far", 1, o), dn)
        elif what == ENDS:
            pl.when(t == 2)(lambda: got(own(WINDOW + 1), ("right",)))
            pl.when(t == 1)(lambda: got(own(WINDOW), ("left",)))
            send(data0.at[far_block, 0, xm, y], ("ends_mate",), mate, condition=inner)
        elif what == ENDS_MATE:
            pl.when(inner)(lambda: got(data0.at[far_block, 0, 1 - xm, y], ("ends_mate",)))
            spread_ends(0)
        elif what == ENDS_Z:
            pl.when(inner)(lambda: got(ends(o, y), ("ends_z", o)))
            spread_ends(o)
        elif what == ENDS_Y:
            for g in range(GROUPS):
                for n, device in enumerate((up, dn, opposite)):
                    send(ends_all(g, y), ("ends", n, g), device, condition=inner)
            tables_from_afar()
        elif what == COMPLETE:
            finish(o)
        elif what == FOCUS:
            if o not in complete:
                complete.add(o)
                got(data[o].at[WINDOW + core], ("core", o))
            if more[0] == 1:
                weights_from_afar()
            if len(complete) == GROUPS and not told:
                pl.semaphore_signal(ready, inc=1, device_id=partner, device_id_type=MESH)
                told.append(True)
            focus(o, more[0])
            if o < GROUPS - 1:
                retire()
            if (o, more[0]) == (GROUPS - 1, 1):
                give(1, 0, partner)
                pl.semaphore_wait(ready, 1)
                give(1, 3, (hp + 1, t), hp < NH - 1)
                give(1, 4, (hp - 1, t), hp > 0)
    give(0, 1, (h + 1, t), h < NH - 1)
    give(0, 2, (h - 1, t), h > 0)

    def take(slot):
        got(vol_in.at[slot], ("volume", slot))

    @pl.when(h > 0)
    def _():
        take(3)
        take(1)

    @pl.when(h == 0)
    def _():
        vol_in[1] = jnp.zeros((8, 512), jnp.float32)
        vol_in[3] = jnp.zeros((8, 512), jnp.float32)

    @pl.when(h < NH - 1)
    def _():
        take(4)
        take(2)

    @pl.when(h == NH - 1)
    def _():
        vol_in[2] = jnp.zeros((8, 512), jnp.float32)
        vol_in[4] = jnp.zeros((8, 512), jnp.float32)

    take(0)
    here = vol[0] + vol_in[0]
    below = vol_in[1] + vol_in[3]
    above = vol_in[2] + vol_in[4]
    for part in range(2):
        rows = jnp.concatenate(
            [below[4 * part + 2 : 4 * part + 4], here[4 * part : 4 * part + 4], above[4 * part : 4 * part + 2]], axis=0
        )
        image = jnp.zeros((4, 512), jnp.float32)
        for j in range(5):
            image = image + taps_ref[j] * rows[j : j + 4]
        out_ref[part] = image * (1.0 / math.sqrt(8 * NH))

    retire()
    retire()


def local(pulse_panels, interp_weights, range_blocks, sector_of_panel, layer_cos, layer_sin, ground_cos, ground_sin, height_kernel):
    blocks = jnp.transpose(range_blocks[0], (2, 0, 1))
    f32, bf16, i32 = jnp.float32, jnp.bfloat16, jnp.int32
    ground = (2, 2, NZ, NY, 8, 512)
    return pl.pallas_call(
        kernel,
        out_shape=jax.ShapeDtypeStruct((2, 4, 512), f32),
        in_specs=[pl.BlockSpec(memory_space=pl.ANY)] * 9,
        out_specs=pl.BlockSpec(memory_space=pltpu.VMEM),
        scratch_shapes=[
            pltpu.VMEM((2, 8, WINDOW * 128), bf16),
            pltpu.VMEM((3, 4, 4), i32),
            pltpu.SMEM((3, 4, 4), i32),
            pltpu.SMEM((NH,), i32),
            pltpu.VMEM((4, 8, NH), f32),
            pltpu.VMEM((4, 8, NH), f32),
            pltpu.SMEM((5,), f32),
        ]
        + [pltpu.VMEM((BLOCKS, 2, 2, NY, 16, 128), bf16)] * GROUPS
        + [
            pltpu.VMEM((4, 4, 3, 128, 128), bf16),
            pltpu.VMEM((4, 4, 3, 128, 128), bf16),
            pltpu.VMEM((3, 4, 4), i32),
            pltpu.SMEM((3, 4, 4), i32),
            pltpu.VMEM((4, 8, NH), f32),
            pltpu.VMEM((4, 8, NH), f32),
            pltpu.VMEM((NZ, 2, NY, 8, 512), bf16),
            pltpu.VMEM((NZ, 2, NY, 8, 512), bf16),
            pltpu.VMEM((NZ, 2, NY, 16, 128), i32),
            pltpu.VMEM((2, 16, HALF * 16), bf16),
            pltpu.VMEM((2, 8, 512), f32),
            pltpu.VMEM((5, 8, 512), f32),
            pltpu.SemaphoreType.DMA((N_SEND,)),
            pltpu.SemaphoreType.DMA((N_RECEIVE,)),
            pltpu.SemaphoreType.DMA((N_LOCAL + 1,)),
            pltpu.SemaphoreType.REGULAR,
        ],
        compiler_params=pltpu.CompilerParams(collective_id=0, has_side_effects=True, vmem_limit_bytes=62 << 20),
        name="focus",
    )(
        pulse_panels[0], interp_weights[0], blocks, sector_of_panel,
        jnp.swapaxes(layer_cos, 1, 2), jnp.swapaxes(layer_sin, 1, 2),
        ground_cos.reshape(ground), ground_sin.reshape(ground), height_kernel,
    )


def solution(mesh):
    in_specs = (
        P("height", None, None, "tile"),
        P("height", None, "tile", None, None, None),
        P("height", None, "tile", None),
        P(),
        P("height", None, None),
        P("height", None, None),
        P(None, None, "tile"),
        P(None, None, "tile"),
        P(),
    )
    return jax.shard_map(local, mesh=mesh, in_specs=in_specs, out_specs=P(None, "height", "tile"), check_vma=False)
```
